512 devices in a mesh: row: 16 (over y, core), col: 32 (over z, x).
Axes of the slice: x: 4, y: 8, z: 8, core: 2. Of those that a mesh axis runs over, the one named last changes fastest.
Arguments:
- initial: float32 [16, 64, 64, 576], P('row', 'col'), as said below
- pattern: int32 [16, 64, 9], P('row', 'col'), may hold values from 0 to 1, as said below
- branch: int32 [5], replicated, may hold values from 0 to 1, as said below
Outputs:
- density: float32 [16, 64, 64, 576], P('row', 'col')
- occupation: float32 [5], replicated
The draws below stay inside these ranges and needn't reach their ends.
Inputs may be any that keep to these rules, and one draw needn't show every extreme that they name: pattern[a, b, 4] is 1 for every atom, and pattern[a, b, k] equals pattern[(a + da) mod 16, (b + db) mod 64, 8 - k] with (da, db) = (k // 3 - 1, k % 3 - 1). The block matrix is symmetric: the block of initial at atom ((a + da) mod 16, (b + db) mod 64) and offset 8 - k is the transpose of its block at atom (a, b) and offset k. branch[0] and branch[1] differ.
All inputs are finite; a program needn't handle non-finite values.
Results may differ from the reference program's by a relative error of at most 0.0003.
Values sent between devices are 32-bit elements; how exact they have to be, the bound alone decides.
A program may use at most 64 MiB of HBM per device.

```python
import math
from functools import reduce
import jax
import jax.numpy as jnp
from jax import lax

BLK = 64
ITERS = 5
LA = 16
LB = 64
M = 65536


def draw_branch(key, part):
    key = jax.random.fold_in(key, 37)
    values = jax.random.randint(key, (ITERS,), 0, 2).astype(jnp.int32)
    values = values.at[1].set(1 - values[0])
    return values


def draw_pattern(key, part):
    key = jax.random.fold_in(key, 11)
    coins = jax.random.randint(key, (LA, LB, 9), 0, 4) > 0
    columns = []
    for position in range(9):
        shift_a = position // 3 - 1
        shift_b = position % 3 - 1
        if position == 4:
            columns.append(jnp.ones((LA, LB), dtype=bool))
        elif position > 4:
            columns.append(coins[:, :, position])
        else:
            columns.append(jnp.roll(coins[:, :, 8 - position], (-shift_a, -shift_b), axis=(0, 1)))
    return jnp.stack(columns, axis=-1).astype(jnp.int32)


def draw_initial(key, part):
    key = jax.random.fold_in(key, 23)
    key_off, key_diag = jax.random.split(key)
    spread = 0.3 / math.sqrt(0.75 * 9 * BLK)
    position = (jnp.arange(M, dtype=jnp.float32) / (M - 1)).reshape(LA, LB, BLK)
    raw = jax.random.normal(key_off, (LA, LB, BLK, 9 * BLK), jnp.float32)
    jitter = 0.03 * jax.random.normal(key_diag, (LA, LB, BLK), jnp.float32)
    diagonal_values = 0.15 + 0.7 * position + jitter
    pieces = raw.reshape(LA, LB, BLK, 9, BLK)
    identity = jnp.eye(BLK, dtype=bool)
    blocks = []
    for position_index in range(9):
        shift_a = position_index // 3 - 1
        shift_b = position_index % 3 - 1
        mirrored = jnp.roll(pieces[:, :, :, 8 - position_index, :], (-shift_a, -shift_b), axis=(0, 1))
        joined = (pieces[:, :, :, position_index, :] + jnp.swapaxes(mirrored, 2, 3)) * (spread * 0.70710678)
        if position_index == 4:
            joined = jnp.where(identity[None, None], diagonal_values[:, :, :, None], joined)
        blocks.append(joined)
    return jnp.stack(blocks, axis=3).reshape(LA, LB, BLK, 9 * BLK).astype(jnp.float32)


def setup_inputs(seed: int = 0) -> dict:
    key_of = jax.random.split(jax.random.key(seed), 4)
    return {
        "initial": draw_initial(jax.random.fold_in(key_of[3], 71), 0),
        "pattern": draw_pattern(jax.random.fold_in(key_of[3], 71), 0),
        "branch": draw_branch(jax.random.fold_in(key_of[3], 71), 0),
    }


def offset_of(position):
    return position // 3 - 1, position % 3 - 1


def square_blocks(extended, row_count, col_count):
    block_size = extended.shape[2]
    center = extended[1:row_count + 1, 1:col_count + 1]
    split_view = extended.reshape(row_count + 2, col_count + 2, block_size, 3, 3 * block_size)
    partial_terms = [[] for position in range(9)]
    for source in range(9):
        step_a, step_b = offset_of(source)
        left_block = center[:, :, :, source * block_size:(source + 1) * block_size]
        neighbour = split_view[1 + step_a:1 + step_a + row_count, 1 + step_b:1 + step_b + col_count]
        lowest = max(-1, -1 - step_b)
        highest = min(1, 1 - step_b)
        for reach_a in (-1, 0, 1):
            target_a = step_a + reach_a
            if abs(target_a) > 1:
                continue
            right_block = neighbour[:, :, :, reach_a + 1, (lowest + 1) * block_size:(highest + 2) * block_size]
            product = jnp.einsum("abrk,abkx->abrx", left_block, right_block, precision=lax.Precision.HIGHEST, preferred_element_type=jnp.float32)
            for reach_b in range(lowest, highest + 1):
                target = (target_a + 1) * 3 + (step_b + reach_b + 1)
                column_start = (reach_b - lowest) * block_size
                partial_terms[target].append(product[..., column_start:column_start + block_size])
    return jnp.concatenate([reduce(jnp.add, terms) for terms in partial_terms], axis=-1)


def whole_square(current):
    rows_total = current.shape[0]
    cols_total = current.shape[1]

    def one_row(index):
        above = lax.dynamic_index_in_dim(current, (index + rows_total - 1) % rows_total, 0, keepdims=True)
        middle = lax.dynamic_index_in_dim(current, index, 0, keepdims=True)
        below = lax.dynamic_index_in_dim(current, (index + 1) % rows_total, 0, keepdims=True)
        band = jnp.concatenate([above, middle, below], axis=0)
        extended = jnp.concatenate([band[:, -1:], band, band[:, :1]], axis=1)
        return square_blocks(extended, 1, cols_total)[0]

    return lax.map(one_row, jnp.arange(rows_total, dtype=jnp.int32))


def reference(initial, pattern, branch):
    block_size = initial.shape[2]
    mask = jnp.repeat(pattern.astype(jnp.float32), block_size, axis=2)[:, :, None, :]
    current = initial * mask
    occupations = []
    for iteration in range(ITERS):
        square = whole_square(current)
        updated = jnp.where(branch[iteration] == 0, square, 2.0 * current - square)
        current = updated * mask
        diagonal_sum = jnp.sum(jnp.trace(current[..., 4 * block_size:5 * block_size], axis1=2, axis2=3))
        occupations.append(diagonal_sum / M)
    return current, jnp.stack(occupations)
```

```python
import functools

import jax
import jax.numpy as jnp
from jax import lax
from jax.experimental import pallas as pl
from jax.experimental.pallas import tpu as pltpu
from jax.sharding import PartitionSpec as P

ITERS = 5
BLK = 64
MESH = pl.DeviceIdType.MESH


def split(value):
    high = value.astype(jnp.bfloat16)
    low = (value - high.astype(jnp.float32)).astype(jnp.bfloat16)
    return high, low


def dot(a, b, transposed=False):
    dims = (((1,), (1,)), ((), ())) if transposed else (((1,), (0,)), ((), ()))
    return lax.dot_general(a, b, dims, preferred_element_type=jnp.float32)


def kernel(
    rows,
    cols,
    order,
    branch_ref,
    pattern_ref,
    initial_ref,
    density_ref,
    occupation_ref,
    x,
    hbuf,
    vbuf,
    cbuf,
    masks,
    pair,
    mid_hi,
    mid_lo,
    out_hi,
    out_lo,
    stats,
    reduced,
    h_send,
    h_recv,
    v_send,
    v_recv,
    c_send,
    c_recv,
    r_send,
    r_recv,
):
    row, col = lax.axis_index("row"), lax.axis_index("col")
    left = (row, lax.rem(col + cols - 1, cols))
    right = (row, lax.rem(col + 1, cols))
    top = (lax.rem(row + rows - 1, rows), col)
    bottom = (lax.rem(row + 1, rows), col)

    ys, zs, xs = rows // 2, max(cols // 4, 1), min(cols, 4)
    y, core = row // 2, lax.rem(row, 2)
    z, xx = col // xs, lax.rem(col, xs)

    def member(phase, index):
        if phase == 0:
            return (index * 2 + core, col)
        if phase == 1:
            return (row, index * xs + xx)
        return (y * 2 + index // xs, z * xs + lax.rem(index, xs))

    own = (y, z, core * xs + xx)
    sizes = (ys, zs, 2 * xs)

    barrier = pltpu.get_barrier_semaphore()
    for device in (left, right, top, bottom):
        pl.semaphore_signal(barrier, inc=1, device_id=device, device_id_type=MESH)
    for phase in range(3):
        for step in range(1, sizes[phase]):
            device = member(phase, lax.rem(own[phase] + step, sizes[phase]))
            pl.semaphore_signal(barrier, inc=1, device_id=device, device_id_type=MESH)

    lane = lax.broadcasted_iota(jnp.int32, (BLK, 2 * BLK), 1)
    zero = jnp.zeros((BLK, BLK), jnp.float32)

    def pattern(atom, k):
        return pattern_ref[0, atom, k].astype(jnp.float32)

    for g in range(3):
        k = 3 * g
        masks[g, 0, 0:BLK] = jnp.where(lane < BLK, pattern(0, k), pattern(0, k + 1))
        masks[g, 1, 0:BLK] = jnp.where(lane < BLK, pattern(0, k + 2), 0.0)
        masks[g, 0, BLK : 2 * BLK] = jnp.where(lane < BLK, 0.0, pattern(1, k))
        masks[g, 1, BLK : 2 * BLK] = jnp.where(lane < BLK, pattern(1, k + 1), pattern(1, k + 2))
        base = k * BLK
        first = initial_ref[0, 0, :, base : base + 3 * BLK]
        second = initial_ref[0, 1, :, base : base + 3 * BLK]
        x[0, g, 0, 0:BLK] = first[:, : 2 * BLK] * masks[g, 0, 0:BLK]
        x[0, g, 1, 0:BLK] = jnp.concatenate([first[:, 2 * BLK :], zero], axis=1) * masks[g, 1, 0:BLK]
        x[0, g, 0, BLK : 2 * BLK] = (
            jnp.concatenate([zero, second[:, :BLK]], axis=1) * masks[g, 0, BLK : 2 * BLK]
        )
        x[0, g, 1, BLK : 2 * BLK] = second[:, BLK:] * masks[g, 1, BLK : 2 * BLK]

    def send_h(i, g):
        return [
            pltpu.make_async_remote_copy(
                x.at[i, g, 1, pl.ds(BLK, BLK)],
                hbuf.at[i, 0, g],
                h_send.at[i, 0, g],
                h_recv.at[i, 0, g],
                device_id=right,
                device_id_type=MESH,
            ),
            pltpu.make_async_remote_copy(
                x.at[i, g, 0, pl.ds(0, BLK)],
                hbuf.at[i, 1, g],
                h_send.at[i, 1, g],
                h_recv.at[i, 1, g],
                device_id=left,
                device_id_type=MESH,
            ),
        ]

    def send_v(i):
        return [
            pltpu.make_async_remote_copy(
                x.at[i, 1],
                vbuf.at[i, side],
                v_send.at[i, side],
                v_recv.at[i, side],
                device_id=device,
                device_id_type=MESH,
            )
            for side, device in ((0, bottom), (1, top))
        ]

    def send_c(i):
        return [
            pltpu.make_async_remote_copy(
                hbuf.at[i, side, 1],
                cbuf.at[i, line, side],
                c_send.at[i, line, side],
                c_recv.at[i, line, side],
                device_id=device,
                device_id_type=MESH,
            )
            for line, device in ((0, bottom), (1, top))
            for side in (0, 1)
        ]

    def start(copies):
        for copy in copies:
            copy.start()

    def wait_recv(copies):
        for copy in copies:
            copy.wait_recv()

    def wait_send(copies):
        for copy in copies:
            copy.wait_send()

    wide_zero = jnp.zeros((BLK, 2 * BLK), jnp.bfloat16)
    for ref in (mid_hi, mid_lo):
        for g in range(3):
            base = g * 4 * BLK
            ref[0:BLK, base + 2 * BLK : base + 4 * BLK] = wide_zero
            ref[3 * BLK : 4 * BLK, base : base + 2 * BLK] = wide_zero
    for ref in (out_hi, out_lo):
        for line in range(2):
            ref[line, 0:BLK, 2 * BLK : 4 * BLK] = wide_zero
            ref[line, 3 * BLK : 4 * BLK, 0 : 2 * BLK] = wide_zero
    stats[...] = jnp.zeros_like(stats)

    pl.semaphore_wait(barrier, 4 + sum(size - 1 for size in sizes))

    start(send_h(0, 1))
    start(send_v(0))
    start(send_h(0, 0))
    start(send_h(0, 2))

    r_iota = lax.broadcasted_iota(jnp.int32, (2 * BLK, 2 * BLK), 0)
    l_iota = lax.broadcasted_iota(jnp.int32, (2 * BLK, 2 * BLK), 1)
    s_iota = lax.broadcasted_iota(jnp.int32, (8, 2 * BLK), 0)

    def fold(value):
        return jnp.sum(value, axis=0, keepdims=True)

    def add_stats(i):
        norm = jnp.zeros((2 * BLK, 2 * BLK), jnp.float32)
        for g in range(3):
            for half in range(2):
                norm = norm + x[i, g, half] * x[i, g, half]
        norm = fold(norm)
        trace = fold(
            jnp.where(l_iota == r_iota + BLK, x[i, 1, 0], 0.0)
            + jnp.where(l_iota + BLK == r_iota, x[i, 1, 1], 0.0)
        )
        occupied = jnp.where(branch_ref[i] == 0, norm, 2.0 * trace - norm)
        stats[...] = jnp.where(s_iota == i, occupied, stats[...])

    def own_operands(i):
        for g in range(3):
            for half in range(2):
                high, low = split(x[i, g, half])
                base = g * 4 * BLK + half * 2 * BLK
                pair[0 : 2 * BLK, base : base + 2 * BLK] = high
                pair[2 * BLK : 4 * BLK, base : base + 2 * BLK] = low
                mid_hi[BLK : 3 * BLK, base : base + 2 * BLK] = high
                mid_lo[BLK : 3 * BLK, base : base + 2 * BLK] = low

    def mid_operands(i, g):
        for side in range(2):
            high, low = split(hbuf[i, side, g])
            base = g * 4 * BLK + side * 2 * BLK
            lines = slice(side * 3 * BLK, side * 3 * BLK + BLK)
            mid_hi[lines, base : base + 2 * BLK] = high
            mid_lo[lines, base : base + 2 * BLK] = low

    def vertical_operands(i, line):
        for half in range(2):
            high, low = split(vbuf[i, line, half])
            lanes = slice(half * 2 * BLK, half * 2 * BLK + 2 * BLK)
            out_hi[line, BLK : 3 * BLK, lanes] = high
            out_lo[line, BLK : 3 * BLK, lanes] = low

    def corner_operands(i, line):
        for side in range(2):
            high, low = split(cbuf[i, line, side])
            lanes = slice(side * 2 * BLK, side * 2 * BLK + 2 * BLK)
            lines = slice(side * 3 * BLK, side * 3 * BLK + BLK)
            out_hi[line, lines, lanes] = high
            out_lo[line, lines, lanes] = low

    wide = 4 * BLK

    def square_mid():
        both = dot(pair[...], mid_hi[...], True)
        return both[: 2 * BLK] + both[2 * BLK :] + dot(pair[0 : 2 * BLK], mid_lo[...], True)

    def square_out(line):
        g = 2 * line
        lanes = slice(g * wide, g * wide + wide)
        inner = slice(wide, 2 * wide)
        both = dot(pair[:, lanes], out_hi[line]) + dot(pair[:, inner], mid_hi[:, lanes])
        cross = dot(pair[0 : 2 * BLK, lanes], out_lo[line]) + dot(pair[0 : 2 * BLK, inner], mid_lo[:, lanes])
        return both[: 2 * BLK] + both[2 * BLK :] + cross

    def update(i, g, square):
        results = []
        for half in range(2):
            part = square[:, half * 2 * BLK : half * 2 * BLK + 2 * BLK]
            new = jnp.where(branch_ref[i] == 0, part, 2.0 * x[i, g, half] - part)
            results.append(new * masks[g, half])
        return results

    def store_x(i, g, results):
        for half in range(2):
            x[i + 1, g, half] = results[half]

    def store_out(g, results):
        base = 3 * g * BLK
        density_ref[0, 0, :, base : base + 3 * BLK] = jnp.concatenate(
            [results[0][:BLK], results[1][:BLK, :BLK]], axis=1
        )
        density_ref[0, 1, :, base : base + 3 * BLK] = jnp.concatenate(
            [results[0][BLK:, BLK:], results[1][BLK:]], axis=1
        )

    def reduce_copies(phase):
        return [
            pltpu.make_async_remote_copy(
                reduced.at[phase, own[phase]],
                reduced.at[phase, own[phase]],
                r_send.at[phase, step],
                r_recv.at[phase, step],
                device_id=member(phase, lax.rem(own[phase] + step, sizes[phase])),
                device_id_type=MESH,
            )
            for step in range(1, sizes[phase])
        ]

    def reduce_begin(phase, value):
        reduced[phase, own[phase]] = value
        copies = reduce_copies(phase)
        start(copies)
        return copies

    def reduce_end(phase, copies):
        wait_recv(copies)
        total = reduced[phase, 0]
        for index in range(1, sizes[phase]):
            total = total + reduced[phase, index]
        return total

    def body(i, carry):
        wait_recv(send_h(i, 1))
        start(send_c(i))
        add_stats(i)
        own_operands(i)
        wait_recv(send_h(i, 0))
        wait_recv(send_h(i, 2))
        for g in range(3):
            mid_operands(i, g)
        store_x(i, 1, update(i, 1, square_mid()))
        start(send_h(i + 1, 1))
        start(send_v(i + 1))
        wait_recv(send_v(i))
        wait_recv(send_c(i))
        for line in range(2):
            vertical_operands(i, line)
            corner_operands(i, line)
            store_x(i, 2 * line, update(i, 2 * line, square_out(line)))
            start(send_h(i + 1, 2 * line))
        return carry

    lax.fori_loop(0, ITERS - 1, body, 0)

    last = ITERS - 1
    wait_recv(send_h(last, 1))
    start(send_c(last))
    add_stats(last)
    copies0 = reduce_begin(0, stats[...])
    own_operands(last)
    wait_recv(send_h(last, 0))
    wait_recv(send_h(last, 2))
    for g in range(3):
        mid_operands(last, g)
    store_out(1, update(last, 1, square_mid()))
    copies1 = reduce_begin(1, reduce_end(0, copies0))
    wait_recv(send_v(last))
    wait_recv(send_c(last))
    vertical_operands(last, 0)
    corner_operands(last, 0)
    store_out(0, update(last, 0, square_out(0)))
    copies2 = reduce_begin(2, reduce_end(1, copies1))
    vertical_operands(last, 1)
    corner_operands(last, 1)
    store_out(2, update(last, 2, square_out(1)))
    total = reduce_end(2, copies2)
    for i in range(ITERS):
        occupation_ref[i] = jnp.sum(total[i : i + 1]) / order

    def drain(i, carry):
        for g in range(3):
            wait_send(send_h(i, g))
        wait_send(send_v(i))
        wait_send(send_c(i))
        return carry

    lax.fori_loop(0, ITERS, drain, 0)
    wait_send(copies0)
    wait_send(copies1)
    wait_send(copies2)


def on_device(rows, cols, order, initial, pattern, branch):
    half = 2 * BLK
    wide = 4 * BLK
    sizes = (rows // 2, max(cols // 4, 1), 2 * min(cols, 4))
    slots = max(sizes)
    vmem = pl.BlockSpec(memory_space=pltpu.VMEM)
    smem = pl.BlockSpec(memory_space=pltpu.SMEM)
    dma = pltpu.SemaphoreType.DMA
    return pl.pallas_call(
        functools.partial(kernel, rows, cols, order),
        out_shape=(
            jax.ShapeDtypeStruct(initial.shape, jnp.float32),
            jax.ShapeDtypeStruct((ITERS,), jnp.float32),
        ),
        in_specs=[smem, smem, vmem],
        out_specs=(vmem, smem),
        scratch_shapes=[
            pltpu.VMEM((ITERS, 3, 2, half, half), jnp.float32),
            pltpu.VMEM((ITERS, 2, 3, BLK, half), jnp.float32),
            pltpu.VMEM((ITERS, 2, 2, half, half), jnp.float32),
            pltpu.VMEM((ITERS, 2, 2, BLK, half), jnp.float32),
            pltpu.VMEM((3, 2, half, half), jnp.float32),
            pltpu.VMEM((wide, 3 * wide), jnp.bfloat16),
            pltpu.VMEM((wide, 3 * wide), jnp.bfloat16),
            pltpu.VMEM((wide, 3 * wide), jnp.bfloat16),
            pltpu.VMEM((2, wide, wide), jnp.bfloat16),
            pltpu.VMEM((2, wide, wide), jnp.bfloat16),
            pltpu.VMEM((8, half), jnp.float32),
            pltpu.VMEM((3, slots, 8, half), jnp.float32),
            dma((ITERS, 2, 3)),
            dma((ITERS, 2, 3)),
            dma((ITERS, 2)),
            dma((ITERS, 2)),
            dma((ITERS, 2, 2)),
            dma((ITERS, 2, 2)),
            dma((3, slots)),
            dma((3, slots)),
        ],
        compiler_params=pltpu.CompilerParams(
            collective_id=0, has_side_effects=True, vmem_limit_bytes=32 * 1024 * 1024
        ),
        cost_estimate=pl.CostEstimate(flops=1800000000, bytes_accessed=600000, transcendentals=0),
    )(branch, pattern, initial)


def solution(mesh):
    rows, cols = mesh.shape["row"], mesh.shape["col"]

    def program(initial, pattern, branch):
        order = initial.shape[0] * initial.shape[1] * initial.shape[2]
        return jax.shard_map(
            functools.partial(on_device, rows, cols, float(order)),
            mesh=mesh,
            in_specs=(P("row", "col", None, None), P("row", "col", None), P()),
            out_specs=(P("row", "col", None, None), P()),
            check_vma=False,
        )(initial, pattern, branch)

    return program
```

```python
import functools

import jax
import jax.numpy as jnp
from jax import lax
from jax.experimental import pallas as pl
from jax.experimental.pallas import tpu as pltpu
from jax.sharding import PartitionSpec as P

ITERS = 5
BLK = 64
MESH = pl.DeviceIdType.MESH


def split(value):
    high = value.astype(jnp.bfloat16)
    low = (value - high.astype(jnp.float32)).astype(jnp.bfloat16)
    return high, low


def dot(a, b, transposed=False):
    dims = (((1,), (1,)), ((), ())) if transposed else (((1,), (0,)), ((), ()))
    return lax.dot_general(a, b, dims, preferred_element_type=jnp.float32)


def beside(a, b):
    return jnp.concatenate([a, b], axis=1)


def pack(block):
    return beside(block[: BLK // 2], block[BLK // 2 :])


def unpack(packed):
    return jnp.concatenate([packed[:, :BLK], packed[:, BLK:]], axis=0)


def kernel(
    rows,
    cols,
    order,
    branch_hbm,
    pattern_hbm,
    initial_hbm,
    density_ref,
    occupation_ref,
    branch_ref,
    pattern_ref,
    initial_ref,
    x,
    u,
    m,
    selves,
    hbuf,
    ubuf,
    mbuf,
    sbuf,
    cbuf,
    mask_x,
    mask_u,
    mask_m,
    pair,
    far_hi,
    far_lo,
    near,
    left_side,
    h_pair,
    stats,
    reduced,
    in_sem,
    h_send,
    h_recv,
    u_send,
    u_recv,
    m_send,
    m_recv,
    s_send,
    s_recv,
    c_send,
    c_recv,
    r_send,
    r_recv,
):
    row, col = lax.axis_index("row"), lax.axis_index("col")
    west, east = lax.rem(col + cols - 1, cols), lax.rem(col + 1, cols)
    north, south = lax.rem(row + rows - 1, rows), lax.rem(row + 1, rows)
    two = 2 * BLK

    ys, zs, xs = rows // 2, max(cols // 4, 1), min(cols, 4)
    y, core = row // 2, lax.rem(row, 2)
    z, xx = col // xs, lax.rem(col, xs)

    def member(phase, index):
        if phase == 0:
            return (index * 2 + core, col)
        if phase == 1:
            return (row, index * xs + xx)
        return (y * 2 + index // xs, z * xs + lax.rem(index, xs))

    own = (y, z, core * xs + xx)
    sizes = (ys, zs, 2 * xs)

    barrier = pltpu.get_barrier_semaphore()
    near_devices = [(row, west), (row, east)] + [
        (a, b) for a in (north, south) for b in (col, west, east)
    ]
    for device in near_devices:
        pl.semaphore_signal(barrier, inc=1, device_id=device, device_id_type=MESH)
    inputs = [
        pltpu.make_async_copy(initial_hbm, initial_ref, in_sem.at[0]),
        pltpu.make_async_copy(pattern_hbm, pattern_ref, in_sem.at[1]),
        pltpu.make_async_copy(branch_hbm, branch_ref, in_sem.at[2]),
    ]
    for copy in inputs:
        copy.start()
    for phase in range(3):
        for step in range(1, sizes[phase]):
            device = member(phase, lax.rem(own[phase] + step, sizes[phase]))
            pl.semaphore_signal(barrier, inc=1, device_id=device, device_id_type=MESH)

    far_hi[...] = jnp.zeros_like(far_hi)
    far_lo[...] = jnp.zeros_like(far_lo)
    near[...] = jnp.zeros_like(near)
    left_side[...] = jnp.zeros_like(left_side)
    stats[...] = jnp.zeros_like(stats)
    for copy in inputs:
        copy.wait()

    lane = lax.broadcasted_iota(jnp.int32, (BLK, two), 1)
    low_lanes = lane < BLK
    zero = jnp.zeros((BLK, BLK), jnp.float32)

    def pattern(atom, k):
        return pattern_ref[0, atom, k].astype(jnp.float32)

    for line in range(2):
        k = 6 * line
        mask_x[line, 0, 0:BLK] = jnp.where(low_lanes, pattern(0, k), pattern(0, k + 1))
        mask_x[line, 1, 0:BLK] = jnp.where(low_lanes, pattern(0, k + 2), 0.0)
        mask_x[line, 0, BLK:two] = jnp.where(low_lanes, 0.0, pattern(1, k))
        mask_x[line, 1, BLK:two] = jnp.where(low_lanes, pattern(1, k + 1), pattern(1, k + 2))
        first = initial_ref[0, 0, :, k * BLK : k * BLK + 3 * BLK]
        second = initial_ref[0, 1, :, k * BLK : k * BLK + 3 * BLK]
        x[0, line, 0, 0:BLK] = first[:, :two] * mask_x[line, 0, 0:BLK]
        x[0, line, 1, 0:BLK] = beside(first[:, two:], zero) * mask_x[line, 1, 0:BLK]
        x[0, line, 0, BLK:two] = beside(zero, second[:, :BLK]) * mask_x[line, 0, BLK:two]
        x[0, line, 1, BLK:two] = second[:, BLK:] * mask_x[line, 1, BLK:two]
    mask_u[0:BLK] = jnp.where(low_lanes, pattern(0, 4), pattern(0, 5))
    mask_u[BLK:two] = jnp.where(low_lanes, pattern(1, 3), pattern(1, 4))
    mask_m[...] = jnp.where(low_lanes, pattern(0, 3), pattern(1, 5))
    first = initial_ref[0, 0, :, 3 * BLK : 6 * BLK]
    second = initial_ref[0, 1, :, 3 * BLK : 6 * BLK]
    u[0, 0:BLK] = first[:, BLK:] * mask_u[0:BLK]
    u[0, BLK:two] = second[:, :two] * mask_u[BLK:two]
    m[0] = beside(first[:, :BLK], second[:, two:]) * mask_m[...]

    def remote(source, target, send, recv, device):
        return pltpu.make_async_remote_copy(
            source, target, send, recv, device_id=device, device_id_type=MESH
        )

    def send_h(i):
        return [
            remote(
                x.at[i, :, 1 - side, pl.ds(BLK - side * BLK, BLK)],
                hbuf.at[i, side],
                h_send.at[i, side],
                h_recv.at[i, side],
                (row, east if side == 0 else west),
            )
            for side in range(2)
        ]

    def send_u(i):
        return [
            remote(
                u.at[i],
                ubuf.at[i, line],
                u_send.at[i, line],
                u_recv.at[i, line],
                (south if line == 0 else north, col),
            )
            for line in range(2)
        ]

    def send_m(i):
        return [
            remote(
                m.at[i],
                mbuf.at[i, line],
                m_send.at[i, line],
                m_recv.at[i, line],
                (south if line == 0 else north, col),
            )
            for line in range(2)
        ]

    def send_s(i):
        return [
            remote(
                selves.at[i, 1 - side],
                sbuf.at[i, side],
                s_send.at[i, side],
                s_recv.at[i, side],
                (row, east if side == 0 else west),
            )
            for side in range(2)
        ]

    def send_c(i):
        return [
            remote(
                selves.at[i, 1 - side],
                cbuf.at[i, line, side],
                c_send.at[i, line, side],
                c_recv.at[i, line, side],
                (south if line == 0 else north, east if side == 0 else west),
            )
            for line in range(2)
            for side in range(2)
        ]

    def start(copies):
        for copy in copies:
            copy.start()

    def wait_recv(copies):
        for copy in copies:
            copy.wait_recv()

    def wait_send(copies):
        for copy in copies:
            copy.wait_send()

    def pack_selves(i, value):
        selves[i, 0] = pack(value[:BLK, :BLK])
        selves[i, 1] = pack(value[BLK:, BLK:])

    def start_own(i):
        start(send_c(i))
        start(send_u(i))
        start(send_s(i))

    pack_selves(0, u[0])
    pl.semaphore_wait(barrier, len(near_devices) + sum(size - 1 for size in sizes))
    start(send_h(0))
    start(send_m(0))
    start_own(0)

    r_iota = lax.broadcasted_iota(jnp.int32, (two, two), 0)
    l_iota = lax.broadcasted_iota(jnp.int32, (two, two), 1)
    s_iota = lax.broadcasted_iota(jnp.int32, (8, two), 0)

    def fold(value):
        return jnp.sum(value, axis=0, keepdims=True)

    def add_stats(i):
        norm = u[i] * u[i]
        for line in range(2):
            for half in range(2):
                norm = norm + x[i, line, half] * x[i, line, half]
        norm = fold(norm) + fold(m[i] * m[i])
        trace = fold(jnp.where(l_iota == r_iota, u[i], 0.0))
        occupied = jnp.where(branch_ref[i] == 0, norm, 2.0 * trace - norm)
        stats[...] = jnp.where(s_iota == i, occupied, stats[...])

    u_lanes = slice(2 * two, 3 * two)
    m_lanes = slice(3 * two, 4 * two)

    def x_lanes(line, half=None):
        base = 4 * two * line
        if half is None:
            return slice(base, base + 2 * two)
        return slice(base + half * two, base + half * two + two)

    def set_pair(lines, lanes, value):
        high, low = split(value)
        pair[lines, lanes] = high
        pair[slice(lines.start + two, lines.stop + two), lanes] = low

    def own_operands(i):
        for line in range(2):
            for half in range(2):
                set_pair(slice(0, two), x_lanes(line, half), x[i, line, half])
        set_pair(slice(0, two), u_lanes, u[i])
        edges = m[i]
        set_pair(slice(0, BLK), m_lanes, jnp.where(low_lanes, edges, 0.0))
        set_pair(slice(BLK, two), m_lanes, jnp.where(low_lanes, 0.0, edges))

    def polynomial(i, old, square, mask):
        return jnp.where(branch_ref[i] == 0, square, 2.0 * old - square) * mask

    def next_u(i):
        both = dot(pair[...], pair[...], True)
        square = both[:two, :two] + both[:two, two:] + both[two:, :two]
        return polynomial(i, u[i], square, mask_u[...])

    def own_part(line):
        high = pair[0:two, u_lanes]
        own = dot(beside(high, high), pair[:, x_lanes(line)])
        return own + dot(pair[two : 2 * two, u_lanes], pair[0:two, x_lanes(line)])

    def near_part(i):
        near[0:two, 0:two] = pair[0:two, m_lanes]
        near[0:two, two : 2 * two] = pair[two : 2 * two, m_lanes]
        ml = beside(unpack(sbuf[i, 0]), zero)
        mr = beside(zero, unpack(sbuf[i, 1]))
        for value, lines in ((ml, slice(two, two + BLK)), (mr, slice(two + BLK, 2 * two))):
            high, low = split(value)
            near[lines, 0:two] = high
            near[lines, two : 2 * two] = low
        both = dot(pair[:, u_lanes.start : m_lanes.stop], near[...])
        return both[:two, :two] + both[:two, two:] + both[two:, :two]

    def far_operands(i, line):
        above = ubuf[i, line]
        edges = mbuf[i, line]
        turned = edges.T
        pieces = (
            (0, 0, beside(unpack(cbuf[i, line, 0]), turned[:BLK])),
            (1, 0, beside(edges[:, :BLK], above[:BLK, :BLK])),
            (1, 1, beside(above[:BLK, BLK:], zero)),
            (2, 0, beside(zero, above[BLK:, :BLK])),
            (2, 1, beside(above[BLK:, BLK:], edges[:, BLK:])),
            (3, 1, beside(turned[BLK:], unpack(cbuf[i, line, 1]))),
        )
        for at, half, value in pieces:
            high, low = split(value)
            far_hi[line, at * BLK : at * BLK + BLK, half * two : half * two + two] = high
            far_lo[line, at * BLK : at * BLK + BLK, half * two : half * two + two] = low

    def far_part(line):
        both = dot(pair[:, x_lanes(line)], far_hi[line])
        return both[:two] + both[two:] + dot(pair[0:two, x_lanes(line)], far_lo[line])

    def side_operands():
        for side in range(2):
            lines = slice(side * BLK, side * BLK + BLK)
            high = pair[lines, m_lanes][:, side * BLK : side * BLK + BLK]
            low = pair[slice(two + side * BLK, two + side * BLK + BLK), m_lanes][
                :, side * BLK : side * BLK + BLK
            ]
            left_side[side, 0:BLK] = beside(high, high)
            left_side[side, BLK:two] = beside(low, jnp.zeros_like(low))

    def message_operands(i):
        for side in range(2):
            for line in range(2):
                high, low = split(hbuf[i, side, line])
                h_pair[side, 0:BLK, line * two : line * two + two] = high
                h_pair[side, BLK:two, line * two : line * two + two] = low

    def message_products():
        outer, edge = [], []
        for side in range(2):
            both = dot(left_side[side], h_pair[side])
            outer.append(both[:BLK] + both[BLK:])
            high = slice(side * BLK, side * BLK + BLK)
            low = slice(two + side * BLK, two + side * BLK + BLK)
            links = jnp.concatenate(
                [
                    beside(pair[high, x_lanes(0, side)], pair[high, x_lanes(1, side)]),
                    beside(pair[low, x_lanes(0, side)], pair[low, x_lanes(1, side)]),
                ],
                axis=0,
            )
            both = dot(links, h_pair[side], True)
            edge.append(both[:BLK, :BLK] + both[:BLK, BLK:] + both[BLK:, :BLK])
        return outer, beside(edge[0], edge[1])

    def finish(i, sums, near_sum, emit_x, emit_m):
        outer, edge = message_products()
        for line in range(2):
            for half in range(2):
                square = sums[line][:, half * two : half * two + two]
                extra = outer[half][:, line * two : line * two + two]
                top, low = square[:BLK], square[BLK:]
                if half == 0:
                    top = top + extra
                else:
                    low = low + extra
                square = jnp.concatenate([top, low], axis=0)
                emit_x(line, half, polynomial(i, x[i, line, half], square, mask_x[line, half]))
        square = jnp.where(low_lanes, near_sum[:BLK], near_sum[BLK:]) + edge
        emit_m(polynomial(i, m[i], square, mask_m[...]))

    def reduce_copies(phase):
        steps = sorted(range(1, sizes[phase]), key=lambda step: -min(step, sizes[phase] - step))
        return [
            remote(
                reduced.at[phase, own[phase]],
                reduced.at[phase, own[phase]],
                r_send.at[phase, step],
                r_recv.at[phase, step],
                member(phase, lax.rem(own[phase] + step, sizes[phase])),
            )
            for step in steps
        ]

    def reduce_begin(phase, value):
        reduced[phase, own[phase]] = value
        copies = reduce_copies(phase)
        start(copies)
        return copies

    def reduce_end(phase, copies):
        wait_recv(copies)
        total = reduced[phase, 0]
        for index in range(1, sizes[phase]):
            total = total + reduced[phase, index]
        return total

    def before_message(i):
        sums = [own_part(line) for line in range(2)]
        side_operands()
        wait_recv(send_s(i))
        near_sum = near_part(i)
        wait_recv(send_u(i))
        wait_recv(send_c(i))
        wait_recv(send_m(i))
        for line in range(2):
            far_operands(i, line)
        sums = [sums[line] + far_part(line) for line in range(2)]
        return sums, near_sum

    def body(i, carry):
        own_operands(i)
        fresh = next_u(i)
        u[i + 1] = fresh
        pack_selves(i + 1, fresh)
        start_own(i + 1)
        add_stats(i)
        sums, near_sum = before_message(i)
        wait_recv(send_h(i))
        message_operands(i)

        def emit_x(line, half, value):
            x[i + 1, line, half] = value

        def emit_m(value):
            m[i + 1] = value

        finish(i, sums, near_sum, emit_x, emit_m)
        start(send_h(i + 1))
        start(send_m(i + 1))
        return carry

    lax.fori_loop(0, ITERS - 1, body, 0)

    last = ITERS - 1
    add_stats(last)
    copies0 = reduce_begin(0, stats[...])
    own_operands(last)
    fresh = next_u(last)
    sums, near_sum = before_message(last)
    copies1 = reduce_begin(1, reduce_end(0, copies0))
    wait_recv(send_h(last))
    message_operands(last)
    parts = {}

    def keep_x(line, half, value):
        parts[line, half] = value

    def keep_m(value):
        parts["m"] = value

    finish(last, sums, near_sum, keep_x, keep_m)
    for line in range(2):
        base = 6 * line * BLK
        a, b = parts[line, 0], parts[line, 1]
        density_ref[0, 0, :, base : base + 3 * BLK] = beside(a[:BLK], b[:BLK, :BLK])
        density_ref[0, 1, :, base : base + 3 * BLK] = beside(a[BLK:, BLK:], b[BLK:])
    edges = parts["m"]
    density_ref[0, 0, :, 3 * BLK : 6 * BLK] = beside(edges[:, :BLK], fresh[:BLK])
    density_ref[0, 1, :, 3 * BLK : 6 * BLK] = beside(fresh[BLK:], edges[:, BLK:])
    copies2 = reduce_begin(2, reduce_end(1, copies1))

    def drain(i, carry):
        for copies in (send_h(i), send_m(i), send_u(i), send_s(i), send_c(i)):
            wait_send(copies)
        return carry

    lax.fori_loop(0, ITERS, drain, 0)
    wait_send(copies0)
    wait_send(copies1)
    total = reduce_end(2, copies2)
    for i in range(ITERS):
        occupation_ref[i] = jnp.sum(total[i : i + 1]) / order
    wait_send(copies2)


def on_device(rows, cols, order, initial, pattern, branch):
    two = 2 * BLK
    sizes = (rows // 2, max(cols // 4, 1), 2 * min(cols, 4))
    slots = max(sizes)
    vmem = pl.BlockSpec(memory_space=pltpu.VMEM)
    smem = pl.BlockSpec(memory_space=pltpu.SMEM)
    hbm = pl.BlockSpec(memory_space=pltpu.HBM)
    dma = pltpu.SemaphoreType.DMA
    f32, bf16 = jnp.float32, jnp.bfloat16
    return pl.pallas_call(
        functools.partial(kernel, rows, cols, order),
        out_shape=(
            jax.ShapeDtypeStruct(initial.shape, jnp.float32),
            jax.ShapeDtypeStruct((ITERS,), jnp.float32),
        ),
        in_specs=[hbm, hbm, hbm],
        out_specs=(vmem, smem),
        scratch_shapes=[
            pltpu.SMEM(branch.shape, jnp.int32),
            pltpu.SMEM(pattern.shape, jnp.int32),
            pltpu.VMEM(initial.shape, f32),
            pltpu.VMEM((ITERS, 2, 2, two, two), f32),
            pltpu.VMEM((ITERS, two, two), f32),
            pltpu.VMEM((ITERS, BLK, two), f32),
            pltpu.VMEM((ITERS, 2, BLK // 2, two), f32),
            pltpu.VMEM((ITERS, 2, 2, BLK, two), f32),
            pltpu.VMEM((ITERS, 2, two, two), f32),
            pltpu.VMEM((ITERS, 2, BLK, two), f32),
            pltpu.VMEM((ITERS, 2, BLK // 2, two), f32),
            pltpu.VMEM((ITERS, 2, 2, BLK // 2, two), f32),
            pltpu.VMEM((2, 2, two, two), f32),
            pltpu.VMEM((two, two), f32),
            pltpu.VMEM((BLK, two), f32),
            pltpu.VMEM((2 * two, 6 * two), bf16),
            pltpu.VMEM((2, 2 * two, 2 * two), bf16),
            pltpu.VMEM((2, 2 * two, 2 * two), bf16),
            pltpu.VMEM((2 * two, 2 * two), bf16),
            pltpu.VMEM((2, two, two), bf16),
            pltpu.VMEM((2, two, 2 * two), bf16),
            pltpu.VMEM((8, two), f32),
            pltpu.VMEM((3, slots, 8, two), f32),
            dma((3,)),
            dma((ITERS, 2)),
            dma((ITERS, 2)),
            dma((ITERS, 2)),
            dma((ITERS, 2)),
            dma((ITERS, 2)),
            dma((ITERS, 2)),
            dma((ITERS, 2)),
            dma((ITERS, 2)),
            dma((ITERS, 2, 2)),
            dma((ITERS, 2, 2)),
            dma((3, slots)),
            dma((3, slots)),
        ],
        compiler_params=pltpu.CompilerParams(
            collective_id=0, has_side_effects=True, vmem_limit_bytes=32 * 1024 * 1024
        ),
        cost_estimate=pl.CostEstimate(flops=1800000000, bytes_accessed=600000, transcendentals=0),
    )(branch, pattern, initial)


def solution(mesh):
    rows, cols = mesh.shape["row"], mesh.shape["col"]

    def program(initial, pattern, branch):
        order = initial.shape[0] * initial.shape[1] * initial.shape[2]
        return jax.shard_map(
            functools.partial(on_device, rows, cols, float(order)),
            mesh=mesh,
            in_specs=(P("row", "col", None, None), P("row", "col", None), P()),
            out_specs=(P("row", "col", None, None), P()),
            check_vma=False,
        )(initial, pattern, branch)

    return program
```

```python
import functools

import jax
import jax.numpy as jnp
from jax import lax
from jax.experimental import pallas as pl
from jax.experimental.pallas import tpu as pltpu
from jax.sharding import PartitionSpec as P

ITERS = 5
BLK = 64
MESH = pl.DeviceIdType.MESH


def split(value):
    high = value.astype(jnp.bfloat16)
    low = (value - high.astype(jnp.float32)).astype(jnp.bfloat16)
    return high, low


def dot(a, b, transposed=False):
    dims = (((1,), (1,)), ((), ())) if transposed else (((1,), (0,)), ((), ()))
    return lax.dot_general(a, b, dims, preferred_element_type=jnp.float32)


def beside(a, b):
    return jnp.concatenate([a, b], axis=1)


def pack(block):
    return beside(block[: BLK // 2], block[BLK // 2 :])


def unpack(packed):
    return jnp.concatenate([packed[:, :BLK], packed[:, BLK:]], axis=0)


def kernel(
    rows,
    cols,
    order,
    branch_hbm,
    pattern_hbm,
    initial_hbm,
    density_ref,
    occupation_ref,
    branch_ref,
    pattern_ref,
    initial_ref,
    x,
    u,
    m,
    selves,
    ends,
    cross,
    hbuf,
    ubuf,
    mbuf,
    sbuf,
    cbuf,
    mask_x,
    mask_u,
    mask_m,
    pair,
    far_hi,
    far_lo,
    near,
    left_side,
    h_pair,
    stats,
    reduced,
    in_sem,
    h_send,
    h_recv,
    u_send,
    u_recv,
    m_send,
    m_recv,
    s_send,
    s_recv,
    c_send,
    c_recv,
    r_send,
    r_recv,
):
    row, col = lax.axis_index("row"), lax.axis_index("col")
    west, east = lax.rem(col + cols - 1, cols), lax.rem(col + 1, cols)
    north, south = lax.rem(row + rows - 1, rows), lax.rem(row + 1, rows)
    two = 2 * BLK

    ys, zs, xs = rows // 2, max(cols // 4, 1), min(cols, 4)
    y, core = row // 2, lax.rem(row, 2)
    z, xx = col // xs, lax.rem(col, xs)

    def member(phase, index):
        if phase == 0:
            return (index * 2 + core, col)
        if phase == 1:
            return (row, index * xs + xx)
        return (y * 2 + index // xs, z * xs + lax.rem(index, xs))

    own = (y, z, core * xs + xx)
    sizes = (ys, zs, 2 * xs)

    barrier = pltpu.get_barrier_semaphore()
    near_devices = [(row, west), (row, east)] + [
        (a, b) for a in (north, south) for b in (col, west, east)
    ]
    for device in near_devices:
        pl.semaphore_signal(barrier, inc=1, device_id=device, device_id_type=MESH)
    inputs = [
        pltpu.make_async_copy(initial_hbm, initial_ref, in_sem.at[0]),
        pltpu.make_async_copy(pattern_hbm, pattern_ref, in_sem.at[1]),
        pltpu.make_async_copy(branch_hbm, branch_ref, in_sem.at[2]),
    ]
    for copy in inputs:
        copy.start()
    for phase in range(3):
        for step in range(1, sizes[phase]):
            device = member(phase, lax.rem(own[phase] + step, sizes[phase]))
            pl.semaphore_signal(barrier, inc=1, device_id=device, device_id_type=MESH)

    far_hi[...] = jnp.zeros_like(far_hi)
    far_lo[...] = jnp.zeros_like(far_lo)
    near[...] = jnp.zeros_like(near)
    left_side[...] = jnp.zeros_like(left_side)
    stats[...] = jnp.zeros_like(stats)
    for copy in inputs:
        copy.wait()

    lane = lax.broadcasted_iota(jnp.int32, (BLK, two), 1)
    low_lanes = lane < BLK
    zero = jnp.zeros((BLK, BLK), jnp.float32)

    def pattern(atom, k):
        return pattern_ref[0, atom, k].astype(jnp.float32)

    for line in range(2):
        k = 6 * line
        mask_x[line, 0, 0:BLK] = jnp.where(low_lanes, pattern(0, k), pattern(0, k + 1))
        mask_x[line, 1, 0:BLK] = jnp.where(low_lanes, pattern(0, k + 2), 0.0)
        mask_x[line, 0, BLK:two] = jnp.where(low_lanes, 0.0, pattern(1, k))
        mask_x[line, 1, BLK:two] = jnp.where(low_lanes, pattern(1, k + 1), pattern(1, k + 2))
        first = initial_ref[0, 0, :, k * BLK : k * BLK + 3 * BLK]
        second = initial_ref[0, 1, :, k * BLK : k * BLK + 3 * BLK]
        x[0, line, 0, 0:BLK] = first[:, :two] * mask_x[line, 0, 0:BLK]
        x[0, line, 1, 0:BLK] = beside(first[:, two:], zero) * mask_x[line, 1, 0:BLK]
        x[0, line, 0, BLK:two] = beside(zero, second[:, :BLK]) * mask_x[line, 0, BLK:two]
        x[0, line, 1, BLK:two] = second[:, BLK:] * mask_x[line, 1, BLK:two]
    mask_u[0:BLK] = jnp.where(low_lanes, pattern(0, 4), pattern(0, 5))
    mask_u[BLK:two] = jnp.where(low_lanes, pattern(1, 3), pattern(1, 4))
    mask_m[...] = jnp.where(low_lanes, pattern(0, 3), pattern(1, 5))
    first = initial_ref[0, 0, :, 3 * BLK : 6 * BLK]
    second = initial_ref[0, 1, :, 3 * BLK : 6 * BLK]
    u[0, 0:BLK] = first[:, BLK:] * mask_u[0:BLK]
    u[0, BLK:two] = second[:, :two] * mask_u[BLK:two]
    m[0] = beside(first[:, :BLK], second[:, two:]) * mask_m[...]

    def remote(source, target, send, recv, device):
        return pltpu.make_async_remote_copy(
            source, target, send, recv, device_id=device, device_id_type=MESH
        )

    def send_h(i):
        return [
            remote(
                ends.at[i, 1 - side],
                hbuf.at[i, side],
                h_send.at[i, side],
                h_recv.at[i, side],
                (row, east if side == 0 else west),
            )
            for side in range(2)
        ]

    def send_u(i):
        return [
            remote(
                u.at[i],
                ubuf.at[i, line],
                u_send.at[i, line],
                u_recv.at[i, line],
                (south if line == 0 else north, col),
            )
            for line in range(2)
        ]

    def send_m(i):
        return [
            remote(
                cross.at[i, 1 - line],
                mbuf.at[i, line],
                m_send.at[i, line],
                m_recv.at[i, line],
                (south if line == 0 else north, col),
            )
            for line in range(2)
        ]

    def send_s(i):
        return [
            remote(
                selves.at[i, 1 - side],
                sbuf.at[i, side],
                s_send.at[i, side],
                s_recv.at[i, side],
                (row, east if side == 0 else west),
            )
            for side in range(2)
        ]

    def send_c(i):
        return [
            remote(
                selves.at[i, 1 - side],
                cbuf.at[i, line, side],
                c_send.at[i, line, side],
                c_recv.at[i, line, side],
                (south if line == 0 else north, east if side == 0 else west),
            )
            for line in range(2)
            for side in range(2)
        ]

    def start(copies):
        for copy in copies:
            copy.start()

    def wait_recv(copies):
        for copy in copies:
            copy.wait_recv()

    def wait_send(copies):
        for copy in copies:
            copy.wait_send()

    def pack_selves(i, value):
        selves[i, 0] = pack(value[:BLK, :BLK])
        selves[i, 1] = pack(value[BLK:, BLK:])

    def pack_messages(i):
        for atom in range(2):
            lines = slice(atom * BLK, atom * BLK + BLK)
            lanes = slice(BLK - atom * BLK, two - atom * BLK)
            ends[i, atom] = beside(x[i, 0, atom, lines][:, lanes], x[i, 1, atom, lines][:, lanes])
        for line in range(2):
            cross[i, line, 0] = m[i]
            cross[i, line, 1] = jnp.where(low_lanes, x[i, line, 0, 0:BLK], x[i, line, 1, BLK:two])

    def start_own(i):
        start(send_c(i))
        start(send_u(i))
        start(send_s(i))

    pack_selves(0, u[0])
    pack_messages(0)
    pl.semaphore_wait(barrier, len(near_devices) + sum(size - 1 for size in sizes))
    start(send_h(0))
    start(send_m(0))
    start_own(0)

    r_iota = lax.broadcasted_iota(jnp.int32, (two, two), 0)
    l_iota = lax.broadcasted_iota(jnp.int32, (two, two), 1)
    s_iota = lax.broadcasted_iota(jnp.int32, (8, two), 0)

    def fold(value):
        return jnp.sum(value, axis=0, keepdims=True)

    def add_stats(i):
        norm = u[i] * u[i]
        for line in range(2):
            for half in range(2):
                norm = norm + x[i, line, half] * x[i, line, half]
        norm = fold(norm) + fold(m[i] * m[i])
        trace = fold(jnp.where(l_iota == r_iota, u[i], 0.0))
        occupied = jnp.where(branch_ref[i] == 0, norm, 2.0 * trace - norm)
        stats[...] = jnp.where(s_iota == i, occupied, stats[...])

    u_lanes = slice(2 * two, 3 * two)
    m_lanes = slice(3 * two, 4 * two)

    def x_lanes(line, half=None):
        base = 4 * two * line
        if half is None:
            return slice(base, base + 2 * two)
        return slice(base + half * two, base + half * two + two)

    def set_pair(lines, lanes, value):
        high, low = split(value)
        pair[lines, lanes] = high
        pair[slice(lines.start + two, lines.stop + two), lanes] = low

    def own_operands(i):
        for line in range(2):
            for half in range(2):
                set_pair(slice(0, two), x_lanes(line, half), x[i, line, half])
        set_pair(slice(0, two), u_lanes, u[i])
        edges = m[i]
        set_pair(slice(0, BLK), m_lanes, jnp.where(low_lanes, edges, 0.0))
        set_pair(slice(BLK, two), m_lanes, jnp.where(low_lanes, 0.0, edges))

    def polynomial(i, old, square, mask):
        return jnp.where(branch_ref[i] == 0, square, 2.0 * old - square) * mask

    def next_u(i):
        both = dot(pair[...], pair[...], True)
        square = both[:two, :two] + both[:two, two:] + both[two:, :two]
        return polynomial(i, u[i], square, mask_u[...])

    def own_part(line):
        high = pair[0:two, u_lanes]
        own = dot(beside(high, high), pair[:, x_lanes(line)])
        return own + dot(pair[two : 2 * two, u_lanes], pair[0:two, x_lanes(line)])

    def near_part(i):
        near[0:two, 0:two] = pair[0:two, m_lanes]
        near[0:two, two : 2 * two] = pair[two : 2 * two, m_lanes]
        ml = beside(unpack(sbuf[i, 0]), zero)
        mr = beside(zero, unpack(sbuf[i, 1]))
        for value, lines in ((ml, slice(two, two + BLK)), (mr, slice(two + BLK, 2 * two))):
            high, low = split(value)
            near[lines, 0:two] = high
            near[lines, two : 2 * two] = low
        both = dot(pair[:, u_lanes.start : m_lanes.stop], near[...])
        return both[:two, :two] + both[:two, two:] + both[two:, :two]

    def far_operands(i, line):
        above = ubuf[i, line]
        edges = mbuf[i, line, 0]
        turned = edges.T
        diagonal = mbuf[i, line, 1].T
        pieces = (
            (0, 0, beside(unpack(cbuf[i, line, 0]), turned[:BLK])),
            (1, 0, beside(edges[:, :BLK], above[:BLK, :BLK])),
            (1, 1, beside(above[:BLK, BLK:], zero)),
            (2, 0, beside(zero, above[BLK:, :BLK])),
            (2, 1, beside(above[BLK:, BLK:], edges[:, BLK:])),
            (3, 1, beside(turned[BLK:], unpack(cbuf[i, line, 1]))),
        )
        for at, half, value in pieces:
            high, low = split(value)
            far_hi[line, at * BLK : at * BLK + BLK, half * two : half * two + two] = high
            far_lo[line, at * BLK : at * BLK + BLK, half * two : half * two + two] = low
        for side in range(2):
            high, low = split(diagonal[side * BLK : side * BLK + BLK])
            base = line * two + BLK - side * BLK
            h_pair[side, 0:BLK, base : base + BLK] = high
            h_pair[side, BLK:two, base : base + BLK] = low

    def far_part(line):
        both = dot(pair[:, x_lanes(line)], far_hi[line])
        return both[:two] + both[two:] + dot(pair[0:two, x_lanes(line)], far_lo[line])

    def side_operands():
        for side in range(2):
            lines = slice(side * BLK, side * BLK + BLK)
            high = pair[lines, m_lanes][:, side * BLK : side * BLK + BLK]
            low = pair[slice(two + side * BLK, two + side * BLK + BLK), m_lanes][
                :, side * BLK : side * BLK + BLK
            ]
            left_side[side, 0:BLK] = beside(high, high)
            left_side[side, BLK:two] = beside(low, jnp.zeros_like(low))

    def message_operands(i):
        for side in range(2):
            high, low = split(hbuf[i, side])
            for line in range(2):
                base = line * two + side * BLK
                h_pair[side, 0:BLK, base : base + BLK] = high[:, line * BLK : line * BLK + BLK]
                h_pair[side, BLK:two, base : base + BLK] = low[:, line * BLK : line * BLK + BLK]

    def message_products():
        outer, edge = [], []
        for side in range(2):
            both = dot(left_side[side], h_pair[side])
            outer.append(both[:BLK] + both[BLK:])
            high = slice(side * BLK, side * BLK + BLK)
            low = slice(two + side * BLK, two + side * BLK + BLK)
            links = jnp.concatenate(
                [
                    beside(pair[high, x_lanes(0, side)], pair[high, x_lanes(1, side)]),
                    beside(pair[low, x_lanes(0, side)], pair[low, x_lanes(1, side)]),
                ],
                axis=0,
            )
            both = dot(links, h_pair[side], True)
            edge.append(both[:BLK, :BLK] + both[:BLK, BLK:] + both[BLK:, :BLK])
        return outer, beside(edge[0], edge[1])

    def finish(i, sums, near_sum, emit_x, emit_m):
        outer, edge = message_products()
        for line in range(2):
            for half in range(2):
                square = sums[line][:, half * two : half * two + two]
                extra = outer[half][:, line * two : line * two + two]
                top, low = square[:BLK], square[BLK:]
                if half == 0:
                    top = top + extra
                else:
                    low = low + extra
                square = jnp.concatenate([top, low], axis=0)
                emit_x(line, half, polynomial(i, x[i, line, half], square, mask_x[line, half]))
        square = jnp.where(low_lanes, near_sum[:BLK], near_sum[BLK:]) + edge
        emit_m(polynomial(i, m[i], square, mask_m[...]))

    def reduce_copies(phase):
        steps = sorted(range(1, sizes[phase]), key=lambda step: -min(step, sizes[phase] - step))
        return [
            remote(
                reduced.at[phase, own[phase]],
                reduced.at[phase, own[phase]],
                r_send.at[phase, step],
                r_recv.at[phase, step],
                member(phase, lax.rem(own[phase] + step, sizes[phase])),
            )
            for step in steps
        ]

    def gather_stats():
        sums = jnp.sum(stats[...], axis=1, keepdims=True)
        lanes = lax.broadcasted_iota(jnp.int32, (8, two), 1)
        return fold(jnp.where(lanes == s_iota, sums, 0.0))

    def reduce_begin(phase, value):
        reduced[phase, own[phase]] = value
        copies = reduce_copies(phase)
        start(copies)
        return copies

    def reduce_end(phase, copies):
        wait_recv(copies)
        total = reduced[phase, 0]
        for index in range(1, sizes[phase]):
            total = total + reduced[phase, index]
        return total

    def before_message(i):
        sums = [own_part(line) for line in range(2)]
        side_operands()
        wait_recv(send_s(i))
        near_sum = near_part(i)
        wait_recv(send_u(i))
        wait_recv(send_c(i))
        wait_recv(send_m(i))
        for line in range(2):
            far_operands(i, line)
        sums = [sums[line] + far_part(line) for line in range(2)]
        return sums, near_sum

    def body(i, carry):
        own_operands(i)
        fresh = next_u(i)
        u[i + 1] = fresh
        pack_selves(i + 1, fresh)
        start_own(i + 1)
        add_stats(i)
        sums, near_sum = before_message(i)
        wait_recv(send_h(i))
        message_operands(i)

        def emit_x(line, half, value):
            x[i + 1, line, half] = value

        def emit_m(value):
            m[i + 1] = value

        finish(i, sums, near_sum, emit_x, emit_m)
        pack_messages(i + 1)
        start(send_h(i + 1))
        start(send_m(i + 1))
        return carry

    lax.fori_loop(0, ITERS - 1, body, 0)

    last = ITERS - 1
    add_stats(last)
    copies0 = reduce_begin(0, gather_stats())
    own_operands(last)
    fresh = next_u(last)
    sums, near_sum = before_message(last)
    copies1 = reduce_begin(1, reduce_end(0, copies0))
    wait_recv(send_h(last))
    message_operands(last)
    parts = {}

    def keep_x(line, half, value):
        parts[line, half] = value

    def keep_m(value):
        parts["m"] = value

    finish(last, sums, near_sum, keep_x, keep_m)
    for line in range(2):
        base = 6 * line * BLK
        a, b = parts[line, 0], parts[line, 1]
        density_ref[0, 0, :, base : base + 3 * BLK] = beside(a[:BLK], b[:BLK, :BLK])
        density_ref[0, 1, :, base : base + 3 * BLK] = beside(a[BLK:, BLK:], b[BLK:])
    edges = parts["m"]
    density_ref[0, 0, :, 3 * BLK : 6 * BLK] = beside(edges[:, :BLK], fresh[:BLK])
    density_ref[0, 1, :, 3 * BLK : 6 * BLK] = beside(fresh[BLK:], edges[:, BLK:])
    copies2 = reduce_begin(2, reduce_end(1, copies1))

    def drain(i, carry):
        for copies in (send_h(i), send_m(i), send_u(i), send_s(i), send_c(i)):
            wait_send(copies)
        return carry

    lax.fori_loop(0, ITERS, drain, 0)
    wait_send(copies0)
    wait_send(copies1)
    total = reduce_end(2, copies2)
    occupation_ref[...] = total / order
    wait_send(copies2)


def on_device(rows, cols, order, initial, pattern, branch):
    two = 2 * BLK
    sizes = (rows // 2, max(cols // 4, 1), 2 * min(cols, 4))
    slots = max(sizes)
    vmem = pl.BlockSpec(memory_space=pltpu.VMEM)
    hbm = pl.BlockSpec(memory_space=pltpu.HBM)
    dma = pltpu.SemaphoreType.DMA
    f32, bf16 = jnp.float32, jnp.bfloat16
    density, sums = pl.pallas_call(
        functools.partial(kernel, rows, cols, order),
        out_shape=(
            jax.ShapeDtypeStruct(initial.shape, jnp.float32),
            jax.ShapeDtypeStruct((1, 2 * BLK), jnp.float32),
        ),
        in_specs=[hbm, hbm, hbm],
        out_specs=(vmem, vmem),
        scratch_shapes=[
            pltpu.SMEM(branch.shape, jnp.int32),
            pltpu.SMEM(pattern.shape, jnp.int32),
            pltpu.VMEM(initial.shape, f32),
            pltpu.VMEM((ITERS, 2, 2, two, two), f32),
            pltpu.VMEM((ITERS, two, two), f32),
            pltpu.VMEM((ITERS, BLK, two), f32),
            pltpu.VMEM((ITERS, 2, BLK // 2, two), f32),
            pltpu.VMEM((ITERS, 2, BLK, two), f32),
            pltpu.VMEM((ITERS, 2, 2, BLK, two), f32),
            pltpu.VMEM((ITERS, 2, BLK, two), f32),
            pltpu.VMEM((ITERS, 2, two, two), f32),
            pltpu.VMEM((ITERS, 2, 2, BLK, two), f32),
            pltpu.VMEM((ITERS, 2, BLK // 2, two), f32),
            pltpu.VMEM((ITERS, 2, 2, BLK // 2, two), f32),
            pltpu.VMEM((2, 2, two, two), f32),
            pltpu.VMEM((two, two), f32),
            pltpu.VMEM((BLK, two), f32),
            pltpu.VMEM((2 * two, 6 * two), bf16),
            pltpu.VMEM((2, 2 * two, 2 * two), bf16),
            pltpu.VMEM((2, 2 * two, 2 * two), bf16),
            pltpu.VMEM((2 * two, 2 * two), bf16),
            pltpu.VMEM((2, two, two), bf16),
            pltpu.VMEM((2, two, 2 * two), bf16),
            pltpu.VMEM((8, two), f32),
            pltpu.VMEM((3, slots, 1, two), f32),
            dma((3,)),
            dma((ITERS, 2)),
            dma((ITERS, 2)),
            dma((ITERS, 2)),
            dma((ITERS, 2)),
            dma((ITERS, 2)),
            dma((ITERS, 2)),
            dma((ITERS, 2)),
            dma((ITERS, 2)),
            dma((ITERS, 2, 2)),
            dma((ITERS, 2, 2)),
            dma((3, slots)),
            dma((3, slots)),
        ],
        compiler_params=pltpu.CompilerParams(
            collective_id=0, has_side_effects=True, vmem_limit_bytes=63 * 1024 * 1024
        ),
        cost_estimate=pl.CostEstimate(flops=1800000000, bytes_accessed=600000, transcendentals=0),
    )(branch, pattern, initial)
    return density, sums[0, :ITERS]


def solution(mesh):
    rows, cols = mesh.shape["row"], mesh.shape["col"]

    def program(initial, pattern, branch):
        order = initial.shape[0] * initial.shape[1] * initial.shape[2]
        return jax.shard_map(
            functools.partial(on_device, rows, cols, float(order)),
            mesh=mesh,
            in_specs=(P("row", "col", None, None), P("row", "col", None), P()),
            out_specs=(P("row", "col", None, None), P()),
            check_vma=False,
        )(initial, pattern, branch)

    return program
```

```python
import functools

import jax
import jax.numpy as jnp
from jax import lax
from jax.experimental import pallas as pl
from jax.experimental.pallas import tpu as pltpu
from jax.sharding import PartitionSpec as P

ITERS = 5
BLK = 64
MESH = pl.DeviceIdType.MESH


def split(value):
    high = value.astype(jnp.bfloat16)
    low = (value - high.astype(jnp.float32)).astype(jnp.bfloat16)
    return high, low


def dot(a, b, transposed=False):
    dims = (((1,), (1,)), ((), ())) if transposed else (((1,), (0,)), ((), ()))
    return lax.dot_general(a, b, dims, preferred_element_type=jnp.float32)


def beside(a, b):
    return jnp.concatenate([a, b], axis=1)


def pack(block):
    return beside(block[: BLK // 2], block[BLK // 2 :])


def unpack(packed):
    return jnp.concatenate([packed[:, :BLK], packed[:, BLK:]], axis=0)


def kernel(
    rows,
    cols,
    order,
    branch_hbm,
    pattern_hbm,
    initial_hbm,
    density_ref,
    occupation_ref,
    branch_ref,
    pattern_ref,
    initial_ref,
    x,
    u,
    m,
    selves,
    ends,
    cross,
    hbuf,
    ubuf,
    mbuf,
    sbuf,
    cbuf,
    mask_x,
    mask_u,
    mask_m,
    pair,
    far_hi,
    far_lo,
    near,
    left_side,
    h_pair,
    stats,
    reduced,
    in_sem,
    h_send,
    h_recv,
    u_send,
    u_recv,
    m_send,
    m_recv,
    s_send,
    s_recv,
    c_send,
    c_recv,
    r_send,
    r_recv,
):
    row, col = lax.axis_index("row"), lax.axis_index("col")
    west, east = lax.rem(col + cols - 1, cols), lax.rem(col + 1, cols)
    north, south = lax.rem(row + rows - 1, rows), lax.rem(row + 1, rows)
    two = 2 * BLK

    ys, zs, xs = rows // 2, max(cols // 4, 1), min(cols, 4)
    y, core = row // 2, lax.rem(row, 2)
    z, xx = col // xs, lax.rem(col, xs)

    def member(phase, index):
        if phase == 0:
            return (index * 2 + core, col)
        if phase == 1:
            return (row, index * xs + xx)
        return (y * 2 + index // xs, z * xs + lax.rem(index, xs))

    own = (y, z, core * xs + xx)
    sizes = (ys, zs, 2 * xs)

    barrier = pltpu.get_barrier_semaphore()
    near_devices = [(row, west), (row, east)] + [
        (a, b) for a in (north, south) for b in (col, west, east)
    ]
    for device in near_devices:
        pl.semaphore_signal(barrier, inc=1, device_id=device, device_id_type=MESH)
    inputs = [
        pltpu.make_async_copy(initial_hbm, initial_ref, in_sem.at[0]),
        pltpu.make_async_copy(pattern_hbm, pattern_ref, in_sem.at[1]),
        pltpu.make_async_copy(branch_hbm, branch_ref, in_sem.at[2]),
    ]
    for copy in inputs:
        copy.start()
    for phase in range(3):
        for step in range(1, sizes[phase]):
            device = member(phase, lax.rem(own[phase] + step, sizes[phase]))
            pl.semaphore_signal(barrier, inc=1, device_id=device, device_id_type=MESH)

    far_hi[...] = jnp.zeros_like(far_hi)
    far_lo[...] = jnp.zeros_like(far_lo)
    near[...] = jnp.zeros_like(near)
    left_side[...] = jnp.zeros_like(left_side)
    stats[...] = jnp.zeros_like(stats)
    for copy in inputs:
        copy.wait()

    lane = lax.broadcasted_iota(jnp.int32, (BLK, two), 1)
    low_lanes = lane < BLK
    zero = jnp.zeros((BLK, BLK), jnp.float32)

    def pattern(atom, k):
        return pattern_ref[0, atom, k].astype(jnp.float32)

    for line in range(2):
        k = 6 * line
        mask_x[line, 0, 0:BLK] = jnp.where(low_lanes, pattern(0, k), pattern(0, k + 1))
        mask_x[line, 1, 0:BLK] = jnp.where(low_lanes, pattern(0, k + 2), 0.0)
        mask_x[line, 0, BLK:two] = jnp.where(low_lanes, 0.0, pattern(1, k))
        mask_x[line, 1, BLK:two] = jnp.where(low_lanes, pattern(1, k + 1), pattern(1, k + 2))
        first = initial_ref[0, 0, :, k * BLK : k * BLK + 3 * BLK]
        second = initial_ref[0, 1, :, k * BLK : k * BLK + 3 * BLK]
        x[0, line, 0, 0:BLK] = first[:, :two] * mask_x[line, 0, 0:BLK]
        x[0, line, 1, 0:BLK] = beside(first[:, two:], zero) * mask_x[line, 1, 0:BLK]
        x[0, line, 0, BLK:two] = beside(zero, second[:, :BLK]) * mask_x[line, 0, BLK:two]
        x[0, line, 1, BLK:two] = second[:, BLK:] * mask_x[line, 1, BLK:two]
    mask_u[0:BLK] = jnp.where(low_lanes, pattern(0, 4), pattern(0, 5))
    mask_u[BLK:two] = jnp.where(low_lanes, pattern(1, 3), pattern(1, 4))
    mask_m[...] = jnp.where(low_lanes, pattern(0, 3), pattern(1, 5))
    first = initial_ref[0, 0, :, 3 * BLK : 6 * BLK]
    second = initial_ref[0, 1, :, 3 * BLK : 6 * BLK]
    u[0, 0:BLK] = first[:, BLK:] * mask_u[0:BLK]
    u[0, BLK:two] = second[:, :two] * mask_u[BLK:two]
    m[0] = beside(first[:, :BLK], second[:, two:]) * mask_m[...]

    def remote(source, target, send, recv, device):
        return pltpu.make_async_remote_copy(
            source, target, send, recv, device_id=device, device_id_type=MESH
        )

    def send_h(i):
        return [
            remote(
                ends.at[i, 1 - side],
                hbuf.at[i, side],
                h_send.at[i, side],
                h_recv.at[i, side],
                (row, east if side == 0 else west),
            )
            for side in range(2)
        ]

    def send_u(i):
        return [
            remote(
                u.at[i],
                ubuf.at[i, line],
                u_send.at[i, line],
                u_recv.at[i, line],
                (south if line == 0 else north, col),
            )
            for line in range(2)
        ]

    def send_m(i):
        return [
            remote(
                cross.at[i, 1 - line],
                mbuf.at[i, line],
                m_send.at[i, line],
                m_recv.at[i, line],
                (south if line == 0 else north, col),
            )
            for line in range(2)
        ]

    def send_s(i):
        return [
            remote(
                selves.at[i, 1 - side],
                sbuf.at[i, side],
                s_send.at[i, side],
                s_recv.at[i, side],
                (row, east if side == 0 else west),
            )
            for side in range(2)
        ]

    def send_c(i):
        return [
            remote(
                selves.at[i, 1 - side],
                cbuf.at[i, line, side],
                c_send.at[i, line, side],
                c_recv.at[i, line, side],
                (south if line == 0 else north, east if side == 0 else west),
            )
            for line in range(2)
            for side in range(2)
        ]

    def start(copies):
        for copy in copies:
            copy.start()

    def wait_recv(copies):
        for copy in copies:
            copy.wait_recv()

    def wait_send(copies):
        for copy in copies:
            copy.wait_send()

    def pack_selves(i, value):
        selves[i, 0] = pack(value[:BLK, :BLK])
        selves[i, 1] = pack(value[BLK:, BLK:])

    def pack_messages(i):
        for atom in range(2):
            lines = slice(atom * BLK, atom * BLK + BLK)
            lanes = slice(BLK - atom * BLK, two - atom * BLK)
            ends[i, atom] = beside(x[i, 0, atom, lines][:, lanes], x[i, 1, atom, lines][:, lanes])
        for line in range(2):
            cross[i, line, 0] = m[i]
            cross[i, line, 1] = jnp.where(low_lanes, x[i, line, 0, 0:BLK], x[i, line, 1, BLK:two])

    def start_own(i):
        start(send_c(i))
        start(send_u(i))
        start(send_s(i))

    pack_selves(0, u[0])
    pack_messages(0)
    pl.semaphore_wait(barrier, len(near_devices) + sum(size - 1 for size in sizes))
    start(send_h(0))
    start(send_m(0))
    start_own(0)

    r_iota = lax.broadcasted_iota(jnp.int32, (two, two), 0)
    l_iota = lax.broadcasted_iota(jnp.int32, (two, two), 1)
    s_iota = lax.broadcasted_iota(jnp.int32, (8, two), 0)

    def fold(value):
        return jnp.sum(value, axis=0, keepdims=True)

    def add_stats(i):
        norm = u[i] * u[i]
        for line in range(2):
            for half in range(2):
                norm = norm + x[i, line, half] * x[i, line, half]
        norm = fold(norm) + fold(m[i] * m[i])
        trace = fold(jnp.where(l_iota == r_iota, u[i], 0.0))
        occupied = jnp.where(branch_ref[i] == 0, norm, 2.0 * trace - norm)
        stats[...] = jnp.where(s_iota == i, occupied, stats[...])

    u_lanes = slice(2 * two, 3 * two)
    m_lanes = slice(3 * two, 4 * two)

    def x_lanes(line, half=None):
        base = 4 * two * line
        if half is None:
            return slice(base, base + 2 * two)
        return slice(base + half * two, base + half * two + two)

    def set_pair(lines, lanes, value):
        high, low = split(value)
        pair[lines, lanes] = high
        pair[slice(lines.start + two, lines.stop + two), lanes] = low

    def own_operands(i):
        for line in range(2):
            for half in range(2):
                set_pair(slice(0, two), x_lanes(line, half), x[i, line, half])
        set_pair(slice(0, two), u_lanes, u[i])
        edges = m[i]
        set_pair(slice(0, BLK), m_lanes, jnp.where(low_lanes, edges, 0.0))
        set_pair(slice(BLK, two), m_lanes, jnp.where(low_lanes, 0.0, edges))

    def polynomial(i, old, square, mask):
        return jnp.where(branch_ref[i] == 0, square, 2.0 * old - square) * mask

    def next_u(i):
        both = dot(pair[...], pair[...], True)
        square = both[:two, :two] + both[:two, two:] + both[two:, :two]
        return polynomial(i, u[i], square, mask_u[...])

    def own_part(line):
        high = pair[0:two, u_lanes]
        own = dot(beside(high, high), pair[:, x_lanes(line)])
        return own + dot(pair[two : 2 * two, u_lanes], pair[0:two, x_lanes(line)])

    def near_part(i):
        near[0:two, 0:two] = pair[0:two, m_lanes]
        near[0:two, two : 2 * two] = pair[two : 2 * two, m_lanes]
        ml = beside(unpack(sbuf[i, 0]), zero)
        mr = beside(zero, unpack(sbuf[i, 1]))
        for value, lines in ((ml, slice(two, two + BLK)), (mr, slice(two + BLK, 2 * two))):
            high, low = split(value)
            near[lines, 0:two] = high
            near[lines, two : 2 * two] = low
        both = dot(pair[:, u_lanes.start : m_lanes.stop], near[...])
        return both[:two, :two] + both[:two, two:] + both[two:, :two]

    def far_operands(i, line):
        above = ubuf[i, line]
        edges = mbuf[i, line, 0]
        turned = edges.T
        diagonal = mbuf[i, line, 1].T
        pieces = (
            (0, 0, beside(unpack(cbuf[i, line, 0]), turned[:BLK])),
            (1, 0, beside(edges[:, :BLK], above[:BLK, :BLK])),
            (1, 1, beside(above[:BLK, BLK:], zero)),
            (2, 0, beside(zero, above[BLK:, :BLK])),
            (2, 1, beside(above[BLK:, BLK:], edges[:, BLK:])),
            (3, 1, beside(turned[BLK:], unpack(cbuf[i, line, 1]))),
        )
        for at, half, value in pieces:
            high, low = split(value)
            far_hi[line, at * BLK : at * BLK + BLK, half * two : half * two + two] = high
            far_lo[line, at * BLK : at * BLK + BLK, half * two : half * two + two] = low
        for side in range(2):
            high, low = split(diagonal[side * BLK : side * BLK + BLK])
            base = line * two + BLK - side * BLK
            h_pair[side, 0:BLK, base : base + BLK] = high
            h_pair[side, BLK:two, base : base + BLK] = low

    def far_part(line):
        both = dot(pair[:, x_lanes(line)], far_hi[line])
        return both[:two] + both[two:] + dot(pair[0:two, x_lanes(line)], far_lo[line])

    def side_operands():
        for side in range(2):
            lines = slice(side * BLK, side * BLK + BLK)
            high = pair[lines, m_lanes][:, side * BLK : side * BLK + BLK]
            low = pair[slice(two + side * BLK, two + side * BLK + BLK), m_lanes][
                :, side * BLK : side * BLK + BLK
            ]
            left_side[side, 0:BLK] = beside(high, high)
            left_side[side, BLK:two] = beside(low, jnp.zeros_like(low))

    def message_operands(i):
        for side in range(2):
            high, low = split(hbuf[i, side])
            for line in range(2):
                base = line * two + side * BLK
                h_pair[side, 0:BLK, base : base + BLK] = high[:, line * BLK : line * BLK + BLK]
                h_pair[side, BLK:two, base : base + BLK] = low[:, line * BLK : line * BLK + BLK]

    def message_products():
        outer, edge = [], []
        for side in range(2):
            both = dot(left_side[side], h_pair[side])
            outer.append(both[:BLK] + both[BLK:])
            high = slice(side * BLK, side * BLK + BLK)
            low = slice(two + side * BLK, two + side * BLK + BLK)
            links = jnp.concatenate(
                [
                    beside(pair[high, x_lanes(0, side)], pair[high, x_lanes(1, side)]),
                    beside(pair[low, x_lanes(0, side)], pair[low, x_lanes(1, side)]),
                ],
                axis=0,
            )
            both = dot(links, h_pair[side], True)
            edge.append(both[:BLK, :BLK] + both[:BLK, BLK:] + both[BLK:, :BLK])
        return outer, beside(edge[0], edge[1])

    def finish(i, sums, near_sum, emit_x, emit_m):
        outer, edge = message_products()
        for line in range(2):
            for half in range(2):
                square = sums[line][:, half * two : half * two + two]
                extra = outer[half][:, line * two : line * two + two]
                top, low = square[:BLK], square[BLK:]
                if half == 0:
                    top = top + extra
                else:
                    low = low + extra
                square = jnp.concatenate([top, low], axis=0)
                emit_x(line, half, polynomial(i, x[i, line, half], square, mask_x[line, half]))
        square = jnp.where(low_lanes, near_sum[:BLK], near_sum[BLK:]) + edge
        emit_m(polynomial(i, m[i], square, mask_m[...]))

    def reduce_copies(phase):
        steps = sorted(range(1, sizes[phase]), key=lambda step: -min(step, sizes[phase] - step))
        return [
            remote(
                reduced.at[phase, own[phase]],
                reduced.at[phase, own[phase]],
                r_send.at[phase, step],
                r_recv.at[phase, step],
                member(phase, lax.rem(own[phase] + step, sizes[phase])),
            )
            for step in steps
        ]

    def gather_stats():
        sums = jnp.sum(stats[...], axis=1, keepdims=True)
        lanes = lax.broadcasted_iota(jnp.int32, (8, two), 1)
        return fold(jnp.where(lanes == s_iota, sums, 0.0))

    def reduce_begin(phase, value):
        reduced[phase, own[phase]] = value
        copies = reduce_copies(phase)
        start(copies)
        return copies

    def reduce_end(phase, copies):
        wait_recv(copies)
        total = reduced[phase, 0]
        for index in range(1, sizes[phase]):
            total = total + reduced[phase, index]
        return total

    def before_message(i):
        sums = [own_part(line) for line in range(2)]
        side_operands()
        wait_recv(send_s(i))
        near_sum = near_part(i)
        wait_recv(send_u(i))
        wait_recv(send_c(i))
        wait_recv(send_m(i))
        for line in range(2):
            far_operands(i, line)
        sums = [sums[line] + far_part(line) for line in range(2)]
        return sums, near_sum

    def body(i, carry):
        own_operands(i)
        fresh = next_u(i)
        u[i + 1] = fresh
        pack_selves(i + 1, fresh)
        start_own(i + 1)
        add_stats(i)
        sums, near_sum = before_message(i)
        wait_recv(send_h(i))
        message_operands(i)

        def emit_x(line, half, value):
            x[i + 1, line, half] = value

        def emit_m(value):
            m[i + 1] = value

        finish(i, sums, near_sum, emit_x, emit_m)
        pack_messages(i + 1)
        start(send_h(i + 1))
        start(send_m(i + 1))
        return carry

    lax.fori_loop(0, ITERS - 1, body, 0)

    last = ITERS - 1
    add_stats(last)
    copies0 = reduce_begin(0, gather_stats())
    own_operands(last)
    fresh = next_u(last)
    sums, near_sum = before_message(last)
    copies1 = reduce_begin(1, reduce_end(0, copies0))
    wait_recv(send_h(last))
    message_operands(last)
    parts = {}

    def keep_x(line, half, value):
        parts[line, half] = value

    def keep_m(value):
        parts["m"] = value

    finish(last, sums, near_sum, keep_x, keep_m)
    for line in range(2):
        base = 6 * line * BLK
        a, b = parts[line, 0], parts[line, 1]
        density_ref[0, 0, :, base : base + 3 * BLK] = beside(a[:BLK], b[:BLK, :BLK])
        density_ref[0, 1, :, base : base + 3 * BLK] = beside(a[BLK:, BLK:], b[BLK:])
    edges = parts["m"]
    density_ref[0, 0, :, 3 * BLK : 6 * BLK] = beside(edges[:, :BLK], fresh[:BLK])
    density_ref[0, 1, :, 3 * BLK : 6 * BLK] = beside(fresh[BLK:], edges[:, BLK:])
    copies2 = reduce_begin(2, reduce_end(1, copies1))

    def drain(i, carry):
        for copies in (send_h(i), send_m(i), send_u(i), send_s(i), send_c(i)):
            wait_send(copies)
        return carry

    lax.fori_loop(0, ITERS, drain, 0)
    wait_send(copies0)
    wait_send(copies1)
    total = reduce_end(2, copies2)
    occupation_ref[...] = total / order
    wait_send(copies2)


def on_device(rows, cols, order, initial, pattern, branch):
    two = 2 * BLK
    sizes = (rows // 2, max(cols // 4, 1), 2 * min(cols, 4))
    slots = max(sizes)
    vmem = pl.BlockSpec(memory_space=pltpu.VMEM)
    hbm = pl.BlockSpec(memory_space=pltpu.HBM)
    dma = pltpu.SemaphoreType.DMA
    f32, bf16 = jnp.float32, jnp.bfloat16
    initial, pattern, branch = (
        pltpu.with_memory_space_constraint(value, pltpu.HBM) for value in (initial, pattern, branch)
    )
    density, sums = pl.pallas_call(
        functools.partial(kernel, rows, cols, order),
        out_shape=(
            jax.ShapeDtypeStruct(initial.shape, jnp.float32),
            jax.ShapeDtypeStruct((1, 2 * BLK), jnp.float32),
        ),
        in_specs=[hbm, hbm, hbm],
        out_specs=(vmem, vmem),
        scratch_shapes=[
            pltpu.SMEM(branch.shape, jnp.int32),
            pltpu.SMEM(pattern.shape, jnp.int32),
            pltpu.VMEM(initial.shape, f32),
            pltpu.VMEM((ITERS, 2, 2, two, two), f32),
            pltpu.VMEM((ITERS, two, two), f32),
            pltpu.VMEM((ITERS, BLK, two), f32),
            pltpu.VMEM((ITERS, 2, BLK // 2, two), f32),
            pltpu.VMEM((ITERS, 2, BLK, two), f32),
            pltpu.VMEM((ITERS, 2, 2, BLK, two), f32),
            pltpu.VMEM((ITERS, 2, BLK, two), f32),
            pltpu.VMEM((ITERS, 2, two, two), f32),
            pltpu.VMEM((ITERS, 2, 2, BLK, two), f32),
            pltpu.VMEM((ITERS, 2, BLK // 2, two), f32),
            pltpu.VMEM((ITERS, 2, 2, BLK // 2, two), f32),
            pltpu.VMEM((2, 2, two, two), f32),
            pltpu.VMEM((two, two), f32),
            pltpu.VMEM((BLK, two), f32),
            pltpu.VMEM((2 * two, 6 * two), bf16),
            pltpu.VMEM((2, 2 * two, 2 * two), bf16),
            pltpu.VMEM((2, 2 * two, 2 * two), bf16),
            pltpu.VMEM((2 * two, 2 * two), bf16),
            pltpu.VMEM((2, two, two), bf16),
            pltpu.VMEM((2, two, 2 * two), bf16),
            pltpu.VMEM((8, two), f32),
            pltpu.VMEM((3, slots, 1, two), f32),
            dma((3,)),
            dma((ITERS, 2)),
            dma((ITERS, 2)),
            dma((ITERS, 2)),
            dma((ITERS, 2)),
            dma((ITERS, 2)),
            dma((ITERS, 2)),
            dma((ITERS, 2)),
            dma((ITERS, 2)),
            dma((ITERS, 2, 2)),
            dma((ITERS, 2, 2)),
            dma((3, slots)),
            dma((3, slots)),
        ],
        compiler_params=pltpu.CompilerParams(
            collective_id=0, has_side_effects=True, vmem_limit_bytes=32 * 1024 * 1024
        ),
        cost_estimate=pl.CostEstimate(flops=1800000000, bytes_accessed=600000, transcendentals=0),
    )(branch, pattern, initial)
    return density, sums[0, :ITERS]


def solution(mesh):
    rows, cols = mesh.shape["row"], mesh.shape["col"]

    def program(initial, pattern, branch):
        order = initial.shape[0] * initial.shape[1] * initial.shape[2]
        return jax.shard_map(
            functools.partial(on_device, rows, cols, float(order)),
            mesh=mesh,
            in_specs=(P("row", "col", None, None), P("row", "col", None), P()),
            out_specs=(P("row", "col", None, None), P()),
            check_vma=False,
        )(initial, pattern, branch)

    return program
```

```python
import functools

import jax
import jax.numpy as jnp
from jax import lax
from jax.experimental import pallas as pl
from jax.experimental.pallas import tpu as pltpu
from jax.sharding import PartitionSpec as P

ITERS = 5
BLK = 64
MESH = pl.DeviceIdType.MESH


def split(value):
    high = value.astype(jnp.bfloat16)
    low = (value - high.astype(jnp.float32)).astype(jnp.bfloat16)
    return high, low


def dot(a, b, transposed=False):
    dims = (((1,), (1,)), ((), ())) if transposed else (((1,), (0,)), ((), ()))
    return lax.dot_general(a, b, dims, preferred_element_type=jnp.float32)


def beside(a, b):
    return jnp.concatenate([a, b], axis=1)


def pack(block):
    return beside(block[: BLK // 2], block[BLK // 2 :])


def unpack(packed):
    return jnp.concatenate([packed[:, :BLK], packed[:, BLK:]], axis=0)


def kernel(
    rows,
    cols,
    order,
    branch_hbm,
    pattern_hbm,
    initial_hbm,
    density_ref,
    occupation_ref,
    branch_ref,
    pattern_ref,
    initial_ref,
    x,
    u,
    m,
    selves,
    ends,
    cross,
    hbuf,
    ubuf,
    mbuf,
    sbuf,
    cbuf,
    mask_x,
    mask_u,
    mask_m,
    pair,
    far_hi,
    far_lo,
    near,
    left_side,
    h_pair,
    stats,
    reduced,
    in_sem,
    h_send,
    h_recv,
    u_send,
    u_recv,
    m_send,
    m_recv,
    s_send,
    s_recv,
    c_send,
    c_recv,
    r_send,
    r_recv,
):
    row, col = lax.axis_index("row"), lax.axis_index("col")
    west, east = lax.rem(col + cols - 1, cols), lax.rem(col + 1, cols)
    north, south = lax.rem(row + rows - 1, rows), lax.rem(row + 1, rows)
    two = 2 * BLK

    def member(phase, index):
        return (index, col) if phase == 0 else (row, index)

    own = (row, col)
    sizes = (rows, cols)

    barrier = pltpu.get_barrier_semaphore()
    near_devices = [(row, west), (row, east)] + [
        (a, b) for a in (north, south) for b in (col, west, east)
    ]
    for device in near_devices:
        pl.semaphore_signal(barrier, inc=1, device_id=device, device_id_type=MESH)
    inputs = [
        pltpu.make_async_copy(initial_hbm, initial_ref, in_sem.at[0]),
        pltpu.make_async_copy(pattern_hbm, pattern_ref, in_sem.at[1]),
        pltpu.make_async_copy(branch_hbm, branch_ref, in_sem.at[2]),
    ]
    for copy in inputs:
        copy.start()
    for phase in range(2):
        for step in range(1, sizes[phase]):
            device = member(phase, lax.rem(own[phase] + step, sizes[phase]))
            pl.semaphore_signal(barrier, inc=1, device_id=device, device_id_type=MESH)

    far_hi[...] = jnp.zeros_like(far_hi)
    far_lo[...] = jnp.zeros_like(far_lo)
    near[...] = jnp.zeros_like(near)
    left_side[...] = jnp.zeros_like(left_side)
    stats[...] = jnp.zeros_like(stats)
    for copy in inputs:
        copy.wait()

    lane = lax.broadcasted_iota(jnp.int32, (BLK, two), 1)
    low_lanes = lane < BLK
    zero = jnp.zeros((BLK, BLK), jnp.float32)

    def pattern(atom, k):
        return pattern_ref[0, atom, k].astype(jnp.float32)

    for line in range(2):
        k = 6 * line
        mask_x[line, 0, 0:BLK] = jnp.where(low_lanes, pattern(0, k), pattern(0, k + 1))
        mask_x[line, 1, 0:BLK] = jnp.where(low_lanes, pattern(0, k + 2), 0.0)
        mask_x[line, 0, BLK:two] = jnp.where(low_lanes, 0.0, pattern(1, k))
        mask_x[line, 1, BLK:two] = jnp.where(low_lanes, pattern(1, k + 1), pattern(1, k + 2))
        first = initial_ref[0, 0, :, k * BLK : k * BLK + 3 * BLK]
        second = initial_ref[0, 1, :, k * BLK : k * BLK + 3 * BLK]
        x[0, line, 0, 0:BLK] = first[:, :two] * mask_x[line, 0, 0:BLK]
        x[0, line, 1, 0:BLK] = beside(first[:, two:], zero) * mask_x[line, 1, 0:BLK]
        x[0, line, 0, BLK:two] = beside(zero, second[:, :BLK]) * mask_x[line, 0, BLK:two]
        x[0, line, 1, BLK:two] = second[:, BLK:] * mask_x[line, 1, BLK:two]
    mask_u[0:BLK] = jnp.where(low_lanes, pattern(0, 4), pattern(0, 5))
    mask_u[BLK:two] = jnp.where(low_lanes, pattern(1, 3), pattern(1, 4))
    mask_m[...] = jnp.where(low_lanes, pattern(0, 3), pattern(1, 5))
    first = initial_ref[0, 0, :, 3 * BLK : 6 * BLK]
    second = initial_ref[0, 1, :, 3 * BLK : 6 * BLK]
    u[0, 0:BLK] = first[:, BLK:] * mask_u[0:BLK]
    u[0, BLK:two] = second[:, :two] * mask_u[BLK:two]
    m[0] = beside(first[:, :BLK], second[:, two:]) * mask_m[...]

    def remote(source, target, send, recv, device):
        return pltpu.make_async_remote_copy(
            source, target, send, recv, device_id=device, device_id_type=MESH
        )

    def send_h(i):
        return [
            remote(
                ends.at[i, 1 - side],
                hbuf.at[i, side],
                h_send.at[i, side],
                h_recv.at[i, side],
                (row, east if side == 0 else west),
            )
            for side in range(2)
        ]

    def send_u(i):
        return [
            remote(
                u.at[i],
                ubuf.at[i, line],
                u_send.at[i, line],
                u_recv.at[i, line],
                (south if line == 0 else north, col),
            )
            for line in range(2)
        ]

    def send_m(i):
        return [
            remote(
                cross.at[i, 1 - line],
                mbuf.at[i, line],
                m_send.at[i, line],
                m_recv.at[i, line],
                (south if line == 0 else north, col),
            )
            for line in range(2)
        ]

    def send_s(i):
        return [
            remote(
                selves.at[i, 1 - side],
                sbuf.at[i, side],
                s_send.at[i, side],
                s_recv.at[i, side],
                (row, east if side == 0 else west),
            )
            for side in range(2)
        ]

    def send_c(i):
        return [
            remote(
                selves.at[i, 1 - side],
                cbuf.at[i, line, side],
                c_send.at[i, line, side],
                c_recv.at[i, line, side],
                (south if line == 0 else north, east if side == 0 else west),
            )
            for line in range(2)
            for side in range(2)
        ]

    def start(copies):
        for copy in copies:
            copy.start()

    def wait_recv(copies):
        for copy in copies:
            copy.wait_recv()

    def wait_send(copies):
        for copy in copies:
            copy.wait_send()

    def pack_selves(i, value):
        selves[i, 0] = pack(value[:BLK, :BLK])
        selves[i, 1] = pack(value[BLK:, BLK:])

    def pack_ends(i):
        for atom in range(2):
            lines = slice(atom * BLK, atom * BLK + BLK)
            lanes = slice(BLK - atom * BLK, two - atom * BLK)
            ends[i, atom] = beside(x[i, 0, atom, lines][:, lanes], x[i, 1, atom, lines][:, lanes])

    def pack_cross(i):
        for line in range(2):
            cross[i, line, 0] = m[i]
            cross[i, line, 1] = jnp.where(low_lanes, x[i, line, 0, 0:BLK], x[i, line, 1, BLK:two])

    def start_own(i):
        start(send_c(i))
        start(send_u(i))
        start(send_s(i))

    pack_selves(0, u[0])
    pack_ends(0)
    pack_cross(0)
    pl.semaphore_wait(barrier, len(near_devices) + sum(size - 1 for size in sizes))
    start(send_h(0))
    start(send_m(0))
    start_own(0)

    r_iota = lax.broadcasted_iota(jnp.int32, (two, two), 0)
    l_iota = lax.broadcasted_iota(jnp.int32, (two, two), 1)
    s_iota = lax.broadcasted_iota(jnp.int32, (8, two), 0)

    def fold(value):
        return jnp.sum(value, axis=0, keepdims=True)

    def add_stats(i):
        norm = u[i] * u[i]
        for line in range(2):
            for half in range(2):
                norm = norm + x[i, line, half] * x[i, line, half]
        norm = fold(norm) + fold(m[i] * m[i])
        trace = fold(jnp.where(l_iota == r_iota, u[i], 0.0))
        occupied = jnp.where(branch_ref[i] == 0, norm, 2.0 * trace - norm)
        stats[...] = jnp.where(s_iota == i, occupied, stats[...])

    u_lanes = slice(2 * two, 3 * two)
    m_lanes = slice(3 * two, 4 * two)

    def x_lanes(line, half=None):
        base = 4 * two * line
        if half is None:
            return slice(base, base + 2 * two)
        return slice(base + half * two, base + half * two + two)

    def set_pair(lines, lanes, value):
        high, low = split(value)
        pair[lines, lanes] = high
        pair[slice(lines.start + two, lines.stop + two), lanes] = low

    def own_operands(i):
        for line in range(2):
            for half in range(2):
                set_pair(slice(0, two), x_lanes(line, half), x[i, line, half])
        set_pair(slice(0, two), u_lanes, u[i])
        edges = m[i]
        set_pair(slice(0, BLK), m_lanes, jnp.where(low_lanes, edges, 0.0))
        set_pair(slice(BLK, two), m_lanes, jnp.where(low_lanes, 0.0, edges))

    def polynomial(i, old, square, mask):
        return jnp.where(branch_ref[i] == 0, square, 2.0 * old - square) * mask

    def next_u(i):
        both = dot(pair[...], pair[...], True)
        square = both[:two, :two] + both[:two, two:] + both[two:, :two]
        return polynomial(i, u[i], square, mask_u[...])

    def own_part(line):
        high = pair[0:two, u_lanes]
        own = dot(beside(high, high), pair[:, x_lanes(line)])
        return own + dot(pair[two : 2 * two, u_lanes], pair[0:two, x_lanes(line)])

    def near_part(i):
        near[0:two, 0:two] = pair[0:two, m_lanes]
        near[0:two, two : 2 * two] = pair[two : 2 * two, m_lanes]
        ml = beside(unpack(sbuf[i, 0]), zero)
        mr = beside(zero, unpack(sbuf[i, 1]))
        for value, lines in ((ml, slice(two, two + BLK)), (mr, slice(two + BLK, 2 * two))):
            high, low = split(value)
            near[lines, 0:two] = high
            near[lines, two : 2 * two] = low
        both = dot(pair[:, u_lanes.start : m_lanes.stop], near[...])
        return both[:two, :two] + both[:two, two:] + both[two:, :two]

    def far_operands(i, line):
        above = ubuf[i, line]
        edges = mbuf[i, line, 0]
        turned = edges.T
        diagonal = mbuf[i, line, 1].T
        pieces = (
            (0, 0, beside(unpack(cbuf[i, line, 0]), turned[:BLK])),
            (1, 0, beside(edges[:, :BLK], above[:BLK, :BLK])),
            (1, 1, beside(above[:BLK, BLK:], zero)),
            (2, 0, beside(zero, above[BLK:, :BLK])),
            (2, 1, beside(above[BLK:, BLK:], edges[:, BLK:])),
            (3, 1, beside(turned[BLK:], unpack(cbuf[i, line, 1]))),
        )
        for at, half, value in pieces:
            high, low = split(value)
            far_hi[line, at * BLK : at * BLK + BLK, half * two : half * two + two] = high
            far_lo[line, at * BLK : at * BLK + BLK, half * two : half * two + two] = low
        for side in range(2):
            high, low = split(diagonal[side * BLK : side * BLK + BLK])
            base = line * two + BLK - side * BLK
            h_pair[side, 0:BLK, base : base + BLK] = high
            h_pair[side, BLK:two, base : base + BLK] = low

    def far_part(line):
        both = dot(pair[:, x_lanes(line)], far_hi[line])
        return both[:two] + both[two:] + dot(pair[0:two, x_lanes(line)], far_lo[line])

    def side_operands():
        for side in range(2):
            lines = slice(side * BLK, side * BLK + BLK)
            high = pair[lines, m_lanes][:, side * BLK : side * BLK + BLK]
            low = pair[slice(two + side * BLK, two + side * BLK + BLK), m_lanes][
                :, side * BLK : side * BLK + BLK
            ]
            left_side[side, 0:BLK] = beside(high, high)
            left_side[side, BLK:two] = beside(low, jnp.zeros_like(low))

    def message_operands(i):
        for side in range(2):
            high, low = split(hbuf[i, side])
            for line in range(2):
                base = line * two + side * BLK
                h_pair[side, 0:BLK, base : base + BLK] = high[:, line * BLK : line * BLK + BLK]
                h_pair[side, BLK:two, base : base + BLK] = low[:, line * BLK : line * BLK + BLK]

    def outer_products():
        outer = []
        for side in range(2):
            both = dot(left_side[side], h_pair[side])
            outer.append(both[:BLK] + both[BLK:])
        return outer

    def edge_products():
        edge = []
        for side in range(2):
            high = slice(side * BLK, side * BLK + BLK)
            low = slice(two + side * BLK, two + side * BLK + BLK)
            links = jnp.concatenate(
                [
                    beside(pair[high, x_lanes(0, side)], pair[high, x_lanes(1, side)]),
                    beside(pair[low, x_lanes(0, side)], pair[low, x_lanes(1, side)]),
                ],
                axis=0,
            )
            both = dot(links, h_pair[side], True)
            edge.append(both[:BLK, :BLK] + both[:BLK, BLK:] + both[BLK:, :BLK])
        return beside(edge[0], edge[1])

    def finish_x(i, sums, emit_x):
        outer = outer_products()
        for line in range(2):
            for half in range(2):
                square = sums[line][:, half * two : half * two + two]
                extra = outer[half][:, line * two : line * two + two]
                top, low = square[:BLK], square[BLK:]
                if half == 0:
                    top = top + extra
                else:
                    low = low + extra
                square = jnp.concatenate([top, low], axis=0)
                emit_x(line, half, polynomial(i, x[i, line, half], square, mask_x[line, half]))

    def next_m(i, near_sum):
        square = jnp.where(low_lanes, near_sum[:BLK], near_sum[BLK:]) + edge_products()
        return polynomial(i, m[i], square, mask_m[...])

    def reduce_copies(phase):
        steps = sorted(range(1, sizes[phase]), key=lambda step: -min(step, sizes[phase] - step))
        return [
            remote(
                reduced.at[phase, own[phase]],
                reduced.at[phase, own[phase]],
                r_send.at[phase, step],
                r_recv.at[phase, step],
                member(phase, lax.rem(own[phase] + step, sizes[phase])),
            )
            for step in steps
        ]

    def gather_stats():
        sums = jnp.sum(stats[...], axis=1, keepdims=True)
        lanes = lax.broadcasted_iota(jnp.int32, (8, two), 1)
        return fold(jnp.where(lanes == s_iota, sums, 0.0))

    def reduce_begin(phase, value):
        reduced[phase, own[phase]] = value
        copies = reduce_copies(phase)
        start(copies)
        return copies

    def reduce_end(phase, copies):
        wait_recv(copies)
        total = reduced[phase, 0]
        for index in range(1, sizes[phase]):
            total = total + reduced[phase, index]
        return total

    def before_message(i, between):
        sums = [own_part(line) for line in range(2)]
        side_operands()
        wait_recv(send_s(i))
        near_sum = near_part(i)
        between()
        wait_recv(send_u(i))
        wait_recv(send_c(i))
        wait_recv(send_m(i))
        for line in range(2):
            far_operands(i, line)
        sums = [sums[line] + far_part(line) for line in range(2)]
        return sums, near_sum

    def body(i, carry):
        own_operands(i)
        fresh = next_u(i)
        u[i + 1] = fresh
        pack_selves(i + 1, fresh)
        start_own(i + 1)
        add_stats(i)
        sums, near_sum = before_message(i, lambda: None)
        wait_recv(send_h(i))
        message_operands(i)

        def emit_x(line, half, value):
            x[i + 1, line, half] = value

        finish_x(i, sums, emit_x)
        pack_ends(i + 1)
        start(send_h(i + 1))
        m[i + 1] = next_m(i, near_sum)
        pack_cross(i + 1)
        start(send_m(i + 1))
        return carry

    lax.fori_loop(0, ITERS - 1, body, 0)

    last = ITERS - 1
    add_stats(last)
    copies0 = reduce_begin(0, gather_stats())
    own_operands(last)
    fresh = next_u(last)
    copies1 = []

    def second_phase():
        copies1.extend(reduce_begin(1, reduce_end(0, copies0)))

    sums, near_sum = before_message(last, second_phase)
    wait_recv(send_h(last))
    message_operands(last)
    parts = {}

    def keep_x(line, half, value):
        parts[line, half] = value

    finish_x(last, sums, keep_x)
    for line in range(2):
        base = 6 * line * BLK
        a, b = parts[line, 0], parts[line, 1]
        density_ref[0, 0, :, base : base + 3 * BLK] = beside(a[:BLK], b[:BLK, :BLK])
        density_ref[0, 1, :, base : base + 3 * BLK] = beside(a[BLK:, BLK:], b[BLK:])
    edges = next_m(last, near_sum)
    density_ref[0, 0, :, 3 * BLK : 6 * BLK] = beside(edges[:, :BLK], fresh[:BLK])
    density_ref[0, 1, :, 3 * BLK : 6 * BLK] = beside(fresh[BLK:], edges[:, BLK:])

    def drain(i, carry):
        for copies in (send_h(i), send_m(i), send_u(i), send_s(i), send_c(i)):
            wait_send(copies)
        return carry

    lax.fori_loop(0, ITERS, drain, 0)
    wait_send(copies0)
    total = reduce_end(1, copies1)
    occupation_ref[...] = total / order
    wait_send(copies1)


def on_device(rows, cols, order, initial, pattern, branch):
    two = 2 * BLK
    slots = max(rows, cols)
    vmem = pl.BlockSpec(memory_space=pltpu.VMEM)
    hbm = pl.BlockSpec(memory_space=pltpu.HBM)
    dma = pltpu.SemaphoreType.DMA
    f32, bf16 = jnp.float32, jnp.bfloat16
    initial, pattern, branch = (
        pltpu.with_memory_space_constraint(value, pltpu.HBM) for value in (initial, pattern, branch)
    )
    density, sums = pl.pallas_call(
        functools.partial(kernel, rows, cols, order),
        out_shape=(
            jax.ShapeDtypeStruct(initial.shape, jnp.float32),
            jax.ShapeDtypeStruct((1, 2 * BLK), jnp.float32),
        ),
        in_specs=[hbm, hbm, hbm],
        out_specs=(vmem, vmem),
        scratch_shapes=[
            pltpu.SMEM(branch.shape, jnp.int32),
            pltpu.SMEM(pattern.shape, jnp.int32),
            pltpu.VMEM(initial.shape, f32),
            pltpu.VMEM((ITERS, 2, 2, two, two), f32),
            pltpu.VMEM((ITERS, two, two), f32),
            pltpu.VMEM((ITERS, BLK, two), f32),
            pltpu.VMEM((ITERS, 2, BLK // 2, two), f32),
            pltpu.VMEM((ITERS, 2, BLK, two), f32),
            pltpu.VMEM((ITERS, 2, 2, BLK, two), f32),
            pltpu.VMEM((ITERS, 2, BLK, two), f32),
            pltpu.VMEM((ITERS, 2, two, two), f32),
            pltpu.VMEM((ITERS, 2, 2, BLK, two), f32),
            pltpu.VMEM((ITERS, 2, BLK // 2, two), f32),
            pltpu.VMEM((ITERS, 2, 2, BLK // 2, two), f32),
            pltpu.VMEM((2, 2, two, two), f32),
            pltpu.VMEM((two, two), f32),
            pltpu.VMEM((BLK, two), f32),
            pltpu.VMEM((2 * two, 6 * two), bf16),
            pltpu.VMEM((2, 2 * two, 2 * two), bf16),
            pltpu.VMEM((2, 2 * two, 2 * two), bf16),
            pltpu.VMEM((2 * two, 2 * two), bf16),
            pltpu.VMEM((2, two, two), bf16),
            pltpu.VMEM((2, two, 2 * two), bf16),
            pltpu.VMEM((8, two), f32),
            pltpu.VMEM((2, slots, 1, two), f32),
            dma((3,)),
            dma((ITERS, 2)),
            dma((ITERS, 2)),
            dma((ITERS, 2)),
            dma((ITERS, 2)),
            dma((ITERS, 2)),
            dma((ITERS, 2)),
            dma((ITERS, 2)),
            dma((ITERS, 2)),
            dma((ITERS, 2, 2)),
            dma((ITERS, 2, 2)),
            dma((2, slots)),
            dma((2, slots)),
        ],
        compiler_params=pltpu.CompilerParams(
            collective_id=0, has_side_effects=True, vmem_limit_bytes=32 * 1024 * 1024
        ),
        cost_estimate=pl.CostEstimate(flops=1800000000, bytes_accessed=600000, transcendentals=0),
    )(branch, pattern, initial)
    return density, sums[0, :ITERS]


def solution(mesh):
    rows, cols = mesh.shape["row"], mesh.shape["col"]

    def program(initial, pattern, branch):
        order = initial.shape[0] * initial.shape[1] * initial.shape[2]
        return jax.shard_map(
            functools.partial(on_device, rows, cols, float(order)),
            mesh=mesh,
            in_specs=(P("row", "col", None, None), P("row", "col", None), P()),
            out_specs=(P("row", "col", None, None), P()),
            check_vma=False,
        )(initial, pattern, branch)

    return program
```

```python
import functools

import jax
import jax.numpy as jnp
from jax import lax
from jax.experimental import pallas as pl
from jax.experimental.pallas import tpu as pltpu
from jax.sharding import PartitionSpec as P

ITERS = 5
BLK = 64
MESH = pl.DeviceIdType.MESH


def split(value):
    high = value.astype(jnp.bfloat16)
    low = (value - high.astype(jnp.float32)).astype(jnp.bfloat16)
    return high, low


def dot(a, b, transposed=False):
    dims = (((1,), (1,)), ((), ())) if transposed else (((1,), (0,)), ((), ()))
    return lax.dot_general(a, b, dims, preferred_element_type=jnp.float32)


def beside(a, b):
    return jnp.concatenate([a, b], axis=1)


def pack(block):
    return beside(block[: BLK // 2], block[BLK // 2 :])


def unpack(packed):
    return jnp.concatenate([packed[:, :BLK], packed[:, BLK:]], axis=0)


def kernel(
    rows,
    cols,
    order,
    branch_hbm,
    pattern_hbm,
    initial_hbm,
    density_ref,
    occupation_ref,
    branch_ref,
    pattern_ref,
    initial_ref,
    x,
    u,
    m,
    selves,
    ends,
    cross,
    hbuf,
    ubuf,
    mbuf,
    sbuf,
    cbuf,
    mask_x,
    mask_u,
    mask_m,
    pair,
    far_hi,
    far_lo,
    near,
    left_side,
    h_pair,
    stats,
    reduced,
    in_sem,
    h_send,
    h_recv,
    u_send,
    u_recv,
    m_send,
    m_recv,
    s_send,
    s_recv,
    c_send,
    c_recv,
    r_send,
    r_recv,
):
    row, col = lax.axis_index("row"), lax.axis_index("col")
    west, east = lax.rem(col + cols - 1, cols), lax.rem(col + 1, cols)
    north, south = lax.rem(row + rows - 1, rows), lax.rem(row + 1, rows)
    two = 2 * BLK

    def member(phase, index):
        return (index, col) if phase == 0 else (row, index)

    own = (row, col)
    sizes = (rows, cols)

    barrier = pltpu.get_barrier_semaphore()
    near_devices = [(row, west), (row, east)] + [
        (a, b) for a in (north, south) for b in (col, west, east)
    ]
    for device in near_devices:
        pl.semaphore_signal(barrier, inc=1, device_id=device, device_id_type=MESH)
    inputs = [
        pltpu.make_async_copy(initial_hbm, initial_ref, in_sem.at[0]),
        pltpu.make_async_copy(pattern_hbm, pattern_ref, in_sem.at[1]),
        pltpu.make_async_copy(branch_hbm, branch_ref, in_sem.at[2]),
    ]
    for copy in inputs:
        copy.start()
    for phase in range(2):
        for step in range(1, sizes[phase]):
            device = member(phase, lax.rem(own[phase] + step, sizes[phase]))
            pl.semaphore_signal(barrier, inc=1, device_id=device, device_id_type=MESH)

    far_hi[...] = jnp.zeros_like(far_hi)
    far_lo[...] = jnp.zeros_like(far_lo)
    near[...] = jnp.zeros_like(near)
    left_side[...] = jnp.zeros_like(left_side)
    stats[...] = jnp.zeros_like(stats)
    for copy in inputs:
        copy.wait()

    lane = lax.broadcasted_iota(jnp.int32, (BLK, two), 1)
    low_lanes = lane < BLK
    zero = jnp.zeros((BLK, BLK), jnp.float32)

    def pattern(atom, k):
        return pattern_ref[0, atom, k].astype(jnp.float32)

    for line in range(2):
        k = 6 * line
        mask_x[line, 0, 0:BLK] = jnp.where(low_lanes, pattern(0, k), pattern(0, k + 1))
        mask_x[line, 1, 0:BLK] = jnp.where(low_lanes, pattern(0, k + 2), 0.0)
        mask_x[line, 0, BLK:two] = jnp.where(low_lanes, 0.0, pattern(1, k))
        mask_x[line, 1, BLK:two] = jnp.where(low_lanes, pattern(1, k + 1), pattern(1, k + 2))
        first = initial_ref[0, 0, :, k * BLK : k * BLK + 3 * BLK]
        second = initial_ref[0, 1, :, k * BLK : k * BLK + 3 * BLK]
        x[0, line, 0, 0:BLK] = first[:, :two] * mask_x[line, 0, 0:BLK]
        x[0, line, 1, 0:BLK] = beside(first[:, two:], zero) * mask_x[line, 1, 0:BLK]
        x[0, line, 0, BLK:two] = beside(zero, second[:, :BLK]) * mask_x[line, 0, BLK:two]
        x[0, line, 1, BLK:two] = second[:, BLK:] * mask_x[line, 1, BLK:two]
    mask_u[0:BLK] = jnp.where(low_lanes, pattern(0, 4), pattern(0, 5))
    mask_u[BLK:two] = jnp.where(low_lanes, pattern(1, 3), pattern(1, 4))
    mask_m[...] = jnp.where(low_lanes, pattern(0, 3), pattern(1, 5))
    first = initial_ref[0, 0, :, 3 * BLK : 6 * BLK]
    second = initial_ref[0, 1, :, 3 * BLK : 6 * BLK]
    u[0, 0:BLK] = first[:, BLK:] * mask_u[0:BLK]
    u[0, BLK:two] = second[:, :two] * mask_u[BLK:two]
    m[0] = beside(first[:, :BLK], second[:, two:]) * mask_m[...]

    def remote(source, target, send, recv, device):
        return pltpu.make_async_remote_copy(
            source, target, send, recv, device_id=device, device_id_type=MESH
        )

    def send_h(i):
        return [
            remote(
                ends.at[i, 1 - side],
                hbuf.at[i, side],
                h_send.at[i, side],
                h_recv.at[i, side],
                (row, east if side == 0 else west),
            )
            for side in range(2)
        ]

    def send_u(i):
        return [
            remote(
                u.at[i],
                ubuf.at[i, line],
                u_send.at[i, line],
                u_recv.at[i, line],
                (south if line == 0 else north, col),
            )
            for line in range(2)
        ]

    def send_m(i):
        return [
            remote(
                cross.at[i, 1 - line],
                mbuf.at[i, line],
                m_send.at[i, line],
                m_recv.at[i, line],
                (south if line == 0 else north, col),
            )
            for line in range(2)
        ]

    def send_s(i):
        return [
            remote(
                selves.at[i, 1 - side],
                sbuf.at[i, side],
                s_send.at[i, side],
                s_recv.at[i, side],
                (row, east if side == 0 else west),
            )
            for side in range(2)
        ]

    def send_c(i):
        return [
            remote(
                selves.at[i, 1 - side],
                cbuf.at[i, line, side],
                c_send.at[i, line, side],
                c_recv.at[i, line, side],
                (south if line == 0 else north, east if side == 0 else west),
            )
            for line in range(2)
            for side in range(2)
        ]

    def start(copies):
        for copy in copies:
            copy.start()

    def wait_recv(copies):
        for copy in copies:
            copy.wait_recv()

    def wait_send(copies):
        for copy in copies:
            copy.wait_send()

    def pack_selves(i, value):
        selves[i, 0] = pack(value[:BLK, :BLK])
        selves[i, 1] = pack(value[BLK:, BLK:])

    def pack_ends(i):
        for atom in range(2):
            lines = slice(atom * BLK, atom * BLK + BLK)
            lanes = slice(BLK - atom * BLK, two - atom * BLK)
            ends[i, atom] = beside(x[i, 0, atom, lines][:, lanes], x[i, 1, atom, lines][:, lanes])

    def pack_cross(i):
        for line in range(2):
            cross[i, line, 0] = m[i]
            cross[i, line, 1] = jnp.where(low_lanes, x[i, line, 0, 0:BLK], x[i, line, 1, BLK:two])

    def start_own(i):
        start(send_c(i))
        start(send_u(i))
        start(send_s(i))

    pack_selves(0, u[0])
    pack_ends(0)
    pack_cross(0)
    pl.semaphore_wait(barrier, len(near_devices) + sum(size - 1 for size in sizes))
    start(send_h(0))
    start(send_m(0))
    start_own(0)

    r_iota = lax.broadcasted_iota(jnp.int32, (two, two), 0)
    l_iota = lax.broadcasted_iota(jnp.int32, (two, two), 1)
    s_iota = lax.broadcasted_iota(jnp.int32, (8, two), 0)

    def fold(value):
        return jnp.sum(value, axis=0, keepdims=True)

    def add_stats(i):
        norm = u[i] * u[i]
        for line in range(2):
            for half in range(2):
                norm = norm + x[i, line, half] * x[i, line, half]
        norm = fold(norm) + fold(m[i] * m[i])
        trace = fold(jnp.where(l_iota == r_iota, u[i], 0.0))
        occupied = jnp.where(branch_ref[i] == 0, norm, 2.0 * trace - norm)
        stats[...] = jnp.where(s_iota == i, occupied, stats[...])

    u_lanes = slice(2 * two, 3 * two)
    m_lanes = slice(3 * two, 4 * two)

    def x_lanes(line, half=None):
        base = 4 * two * line
        if half is None:
            return slice(base, base + 2 * two)
        return slice(base + half * two, base + half * two + two)

    def set_pair(lines, lanes, value):
        high, low = split(value)
        pair[lines, lanes] = high
        pair[slice(lines.start + two, lines.stop + two), lanes] = low

    def own_operands(i):
        for line in range(2):
            for half in range(2):
                set_pair(slice(0, two), x_lanes(line, half), x[i, line, half])
        set_pair(slice(0, two), u_lanes, u[i])
        edges = m[i]
        set_pair(slice(0, BLK), m_lanes, jnp.where(low_lanes, edges, 0.0))
        set_pair(slice(BLK, two), m_lanes, jnp.where(low_lanes, 0.0, edges))

    def polynomial(i, old, square, mask):
        return jnp.where(branch_ref[i] == 0, square, 2.0 * old - square) * mask

    def next_u(i):
        both = dot(pair[...], pair[...], True)
        square = both[:two, :two] + both[:two, two:] + both[two:, :two]
        return polynomial(i, u[i], square, mask_u[...])

    def own_part(line):
        high = pair[0:two, u_lanes]
        own = dot(beside(high, high), pair[:, x_lanes(line)])
        return own + dot(pair[two : 2 * two, u_lanes], pair[0:two, x_lanes(line)])

    def near_part(i):
        near[0:two, 0:two] = pair[0:two, m_lanes]
        near[0:two, two : 2 * two] = pair[two : 2 * two, m_lanes]
        ml = beside(unpack(sbuf[i, 0]), zero)
        mr = beside(zero, unpack(sbuf[i, 1]))
        for value, lines in ((ml, slice(two, two + BLK)), (mr, slice(two + BLK, 2 * two))):
            high, low = split(value)
            near[lines, 0:two] = high
            near[lines, two : 2 * two] = low
        both = dot(pair[:, u_lanes.start : m_lanes.stop], near[...])
        return both[:two, :two] + both[:two, two:] + both[two:, :two]

    def far_operands(i, line):
        above = ubuf[i, line]
        edges = mbuf[i, line, 0]
        turned = edges.T
        diagonal = mbuf[i, line, 1].T
        pieces = (
            (0, 0, beside(unpack(cbuf[i, line, 0]), turned[:BLK])),
            (1, 0, beside(edges[:, :BLK], above[:BLK, :BLK])),
            (1, 1, beside(above[:BLK, BLK:], zero)),
            (2, 0, beside(zero, above[BLK:, :BLK])),
            (2, 1, beside(above[BLK:, BLK:], edges[:, BLK:])),
            (3, 1, beside(turned[BLK:], unpack(cbuf[i, line, 1]))),
        )
        for at, half, value in pieces:
            high, low = split(value)
            far_hi[line, at * BLK : at * BLK + BLK, half * two : half * two + two] = high
            far_lo[line, at * BLK : at * BLK + BLK, half * two : half * two + two] = low
        for side in range(2):
            high, low = split(diagonal[side * BLK : side * BLK + BLK])
            base = line * two + BLK - side * BLK
            h_pair[side, 0:BLK, base : base + BLK] = high
            h_pair[side, BLK:two, base : base + BLK] = low

    def far_part(line):
        both = dot(pair[:, x_lanes(line)], far_hi[line])
        return both[:two] + both[two:] + dot(pair[0:two, x_lanes(line)], far_lo[line])

    def side_operands():
        for side in range(2):
            lines = slice(side * BLK, side * BLK + BLK)
            high = pair[lines, m_lanes][:, side * BLK : side * BLK + BLK]
            low = pair[slice(two + side * BLK, two + side * BLK + BLK), m_lanes][
                :, side * BLK : side * BLK + BLK
            ]
            left_side[side, 0:BLK] = beside(high, high)
            left_side[side, BLK:two] = beside(low, jnp.zeros_like(low))

    def message_operands(i):
        for side in range(2):
            high, low = split(hbuf[i, side])
            for line in range(2):
                base = line * two + side * BLK
                h_pair[side, 0:BLK, base : base + BLK] = high[:, line * BLK : line * BLK + BLK]
                h_pair[side, BLK:two, base : base + BLK] = low[:, line * BLK : line * BLK + BLK]

    def outer_products():
        outer = []
        for side in range(2):
            both = dot(left_side[side], h_pair[side])
            outer.append(both[:BLK] + both[BLK:])
        return outer

    def edge_products():
        edge = []
        for side in range(2):
            high = slice(side * BLK, side * BLK + BLK)
            low = slice(two + side * BLK, two + side * BLK + BLK)
            links = jnp.concatenate(
                [
                    beside(pair[high, x_lanes(0, side)], pair[high, x_lanes(1, side)]),
                    beside(pair[low, x_lanes(0, side)], pair[low, x_lanes(1, side)]),
                ],
                axis=0,
            )
            both = dot(links, h_pair[side], True)
            edge.append(both[:BLK, :BLK] + both[:BLK, BLK:] + both[BLK:, :BLK])
        return beside(edge[0], edge[1])

    def finish_x(i, sums, emit_x):
        outer = outer_products()
        for line in range(2):
            for half in range(2):
                square = sums[line][:, half * two : half * two + two]
                extra = outer[half][:, line * two : line * two + two]
                top, low = square[:BLK], square[BLK:]
                if half == 0:
                    top = top + extra
                else:
                    low = low + extra
                square = jnp.concatenate([top, low], axis=0)
                emit_x(line, half, polynomial(i, x[i, line, half], square, mask_x[line, half]))

    def next_m(i, near_sum):
        square = jnp.where(low_lanes, near_sum[:BLK], near_sum[BLK:]) + edge_products()
        return polynomial(i, m[i], square, mask_m[...])

    def reduce_copies(phase):
        steps = sorted(range(1, sizes[phase]), key=lambda step: -min(step, sizes[phase] - step))
        return [
            remote(
                reduced.at[phase, own[phase]],
                reduced.at[phase, own[phase]],
                r_send.at[phase, step],
                r_recv.at[phase, step],
                member(phase, lax.rem(own[phase] + step, sizes[phase])),
            )
            for step in steps
        ]

    def gather_stats():
        sums = jnp.sum(stats[...], axis=1, keepdims=True)
        lanes = lax.broadcasted_iota(jnp.int32, (8, two), 1)
        return fold(jnp.where(lanes == s_iota, sums, 0.0))

    def reduce_begin(phase, value):
        reduced[phase, own[phase]] = value
        copies = reduce_copies(phase)
        start(copies)
        return copies

    def reduce_end(phase, copies):
        wait_recv(copies)
        total = reduced[phase, 0]
        for index in range(1, sizes[phase]):
            total = total + reduced[phase, index]
        return total

    def before_message(i, between):
        sums = [own_part(line) for line in range(2)]
        side_operands()
        wait_recv(send_s(i))
        near_sum = near_part(i)
        between()
        wait_recv(send_u(i))
        wait_recv(send_c(i))
        wait_recv(send_m(i))
        for line in range(2):
            far_operands(i, line)
        sums = [sums[line] + far_part(line) for line in range(2)]
        return sums, near_sum

    def step(i, ahead):
        own_operands(i)
        fresh = next_u(i)
        u[i + 1] = fresh
        pack_selves(i + 1, fresh)
        start_own(i + 1)
        add_stats(i)
        sums, near_sum = before_message(i, lambda: None)
        wait_recv(send_h(i))
        message_operands(i)

        def emit_x(line, half, value):
            x[i + 1, line, half] = value

        finish_x(i, sums, emit_x)
        if ahead is None:
            pack_ends(i + 1)
            start(send_h(i + 1))
            m[i + 1] = next_m(i, near_sum)
        else:
            m[i + 1] = next_m(i, near_sum)
            ahead()
            pack_ends(i + 1)
            start(send_h(i + 1))
        pack_cross(i + 1)
        start(send_m(i + 1))

    def body(i, carry):
        step(i, None)
        return carry

    last = ITERS - 1
    copies0 = []

    def first_phase():
        add_stats(last)
        copies0.extend(reduce_begin(0, gather_stats()))

    lax.fori_loop(0, ITERS - 2, body, 0)
    step(ITERS - 2, first_phase)
    own_operands(last)
    fresh = next_u(last)
    copies1 = []

    def second_phase():
        copies1.extend(reduce_begin(1, reduce_end(0, copies0)))

    sums, near_sum = before_message(last, second_phase)
    wait_recv(send_h(last))
    message_operands(last)
    parts = {}

    def keep_x(line, half, value):
        parts[line, half] = value

    finish_x(last, sums, keep_x)
    for line in range(2):
        base = 6 * line * BLK
        a, b = parts[line, 0], parts[line, 1]
        density_ref[0, 0, :, base : base + 3 * BLK] = beside(a[:BLK], b[:BLK, :BLK])
        density_ref[0, 1, :, base : base + 3 * BLK] = beside(a[BLK:, BLK:], b[BLK:])
    edges = next_m(last, near_sum)
    density_ref[0, 0, :, 3 * BLK : 6 * BLK] = beside(edges[:, :BLK], fresh[:BLK])
    density_ref[0, 1, :, 3 * BLK : 6 * BLK] = beside(fresh[BLK:], edges[:, BLK:])

    def drain(i, carry):
        for copies in (send_h(i), send_m(i), send_u(i), send_s(i), send_c(i)):
            wait_send(copies)
        return carry

    lax.fori_loop(0, ITERS, drain, 0)
    wait_send(copies0)
    total = reduce_end(1, copies1)
    occupation_ref[...] = total / order
    wait_send(copies1)


def on_device(rows, cols, order, initial, pattern, branch):
    two = 2 * BLK
    slots = max(rows, cols)
    vmem = pl.BlockSpec(memory_space=pltpu.VMEM)
    hbm = pl.BlockSpec(memory_space=pltpu.HBM)
    dma = pltpu.SemaphoreType.DMA
    f32, bf16 = jnp.float32, jnp.bfloat16
    initial, pattern, branch = (
        pltpu.with_memory_space_constraint(value, pltpu.HBM) for value in (initial, pattern, branch)
    )
    density, sums = pl.pallas_call(
        functools.partial(kernel, rows, cols, order),
        out_shape=(
            jax.ShapeDtypeStruct(initial.shape, jnp.float32),
            jax.ShapeDtypeStruct((1, 2 * BLK), jnp.float32),
        ),
        in_specs=[hbm, hbm, hbm],
        out_specs=(vmem, vmem),
        scratch_shapes=[
            pltpu.SMEM(branch.shape, jnp.int32),
            pltpu.SMEM(pattern.shape, jnp.int32),
            pltpu.VMEM(initial.shape, f32),
            pltpu.VMEM((ITERS, 2, 2, two, two), f32),
            pltpu.VMEM((ITERS, two, two), f32),
            pltpu.VMEM((ITERS, BLK, two), f32),
            pltpu.VMEM((ITERS, 2, BLK // 2, two), f32),
            pltpu.VMEM((ITERS, 2, BLK, two), f32),
            pltpu.VMEM((ITERS, 2, 2, BLK, two), f32),
            pltpu.VMEM((ITERS, 2, BLK, two), f32),
            pltpu.VMEM((ITERS, 2, two, two), f32),
            pltpu.VMEM((ITERS, 2, 2, BLK, two), f32),
            pltpu.VMEM((ITERS, 2, BLK // 2, two), f32),
            pltpu.VMEM((ITERS, 2, 2, BLK // 2, two), f32),
            pltpu.VMEM((2, 2, two, two), f32),
            pltpu.VMEM((two, two), f32),
            pltpu.VMEM((BLK, two), f32),
            pltpu.VMEM((2 * two, 6 * two), bf16),
            pltpu.VMEM((2, 2 * two, 2 * two), bf16),
            pltpu.VMEM((2, 2 * two, 2 * two), bf16),
            pltpu.VMEM((2 * two, 2 * two), bf16),
            pltpu.VMEM((2, two, two), bf16),
            pltpu.VMEM((2, two, 2 * two), bf16),
            pltpu.VMEM((8, two), f32),
            pltpu.VMEM((2, slots, 1, two), f32),
            dma((3,)),
            dma((ITERS, 2)),
            dma((ITERS, 2)),
            dma((ITERS, 2)),
            dma((ITERS, 2)),
            dma((ITERS, 2)),
            dma((ITERS, 2)),
            dma((ITERS, 2)),
            dma((ITERS, 2)),
            dma((ITERS, 2, 2)),
            dma((ITERS, 2, 2)),
            dma((2, slots)),
            dma((2, slots)),
        ],
        compiler_params=pltpu.CompilerParams(
            collective_id=0, has_side_effects=True, vmem_limit_bytes=32 * 1024 * 1024
        ),
        cost_estimate=pl.CostEstimate(flops=1800000000, bytes_accessed=600000, transcendentals=0),
    )(branch, pattern, initial)
    return density, sums[0, :ITERS]


def solution(mesh):
    rows, cols = mesh.shape["row"], mesh.shape["col"]

    def program(initial, pattern, branch):
        order = initial.shape[0] * initial.shape[1] * initial.shape[2]
        return jax.shard_map(
            functools.partial(on_device, rows, cols, float(order)),
            mesh=mesh,
            in_specs=(P("row", "col", None, None), P("row", "col", None), P()),
            out_specs=(P("row", "col", None, None), P()),
            check_vma=False,
        )(initial, pattern, branch)

    return program
```
